32 devices in a mesh: cluster: 4 (over y, x), group: 8 (over z, core).
Axes of the slice: x: 2, y: 2, z: 4, core: 2. Of those that a mesh axis runs over, the one named last changes fastest.
Arguments:
- coeffs: bfloat16 [8192, 480], P(('cluster', 'group')), may hold values from -6 to 6
- t_matrix: float32 [8192, 480], P(('cluster', 'group')), may hold values from -0.7 to 0.7
- trans_table: bfloat16 [32, 480, 480], replicated
- pair_source: int32 [425984], P(('cluster', 'group')), may hold values from 0 to 2047
- pair_owner: int32 [425984, 1], P(('cluster', 'group')), may hold values from 0 to 23; in each aligned block of 13312 rows (0 to 13311, 13312 to 26623, ...) at most 832 rows name the same one
- pair_row: int32 [425984], P(('cluster', 'group')), may hold values from 0 to 255
- block_matrix: int32 [3328], P(('cluster', 'group')), may hold values from 0 to 31
- block_live: int32 [32], P(('cluster', 'group')), may hold values from 52 to 104, as said below
Outputs:
- product: float32 [8192, 480], P(('cluster', 'group'))
The draws below stay inside these ranges and needn't reach their ends.
Inputs may be any that keep to these rules, and one draw needn't show every extreme that they name: `pair_owner`: among the pairs of one device, at most 832 have the same owner slot, and exactly 832 do for some slot in some devices. `block_live`: blocks at or past a device's count are padding and contribute nothing; some device has all 104 blocks live.
All inputs are finite; a program needn't handle non-finite values.
Results may differ from the reference program's by a relative error of at most 0.0027.
Values may be sent and summed in bfloat16 or wider, within the bound.
No kernel may reach another device: no remote copies, remote signals or barrier semaphores. Data moves between devices by JAX's collectives and lax.ppermute only.
A program may use at most 192 MiB of HBM per device.

```python
import math
import jax
import jax.numpy as jnp
import numpy as np
from jax import lax

COEF = 240
DROP_DEV = 256
PAIR_BLOCK = 128
BLK_DEV = 104
MATS = 32
DEVICE_COUNT = 32
DROPLETS = 8192
BLOCKS = 3328
PAIRS = 425984
CAP = 832
N_CLUSTER = 4
N_GROUP = 8


def draw_trans_table(key, part):
    key = jax.random.fold_in(key, 11)
    key_real, key_imag = jax.random.split(key)
    spread = (2.0 * COEF) ** (-0.5)
    real_part = spread * jax.random.normal(key_real, (MATS, COEF, COEF), jnp.float32)
    imag_part = spread * jax.random.normal(key_imag, (MATS, COEF, COEF), jnp.float32)
    upper_half = jnp.concatenate([real_part, imag_part], axis=2)
    lower_half = jnp.concatenate([-imag_part, real_part], axis=2)
    return jnp.concatenate([upper_half, lower_half], axis=1).astype(jnp.bfloat16)


def draw_block_live(key, part):
    key = jax.random.fold_in(key, 23)
    counts = jax.random.randint(key, (DEVICE_COUNT,), BLK_DEV // 2, BLK_DEV + 1, jnp.int32)
    fullest = jax.random.randint(jax.random.fold_in(key, 5), (), 0, DEVICE_COUNT, jnp.int32)
    return counts.at[fullest].set(BLK_DEV)


def place_ends(entries, stream_key, least, high):
    spot = [jax.random.randint(jax.random.fold_in(stream_key, axis), (), 0, length) for axis, length in enumerate(entries.shape)]
    widest = entries.shape.index(max(entries.shape))
    beside = spot[:widest] + [(spot[widest] + 1) % entries.shape[widest]] + spot[widest + 1:]
    return entries.at[tuple(spot)].set(least).at[tuple(beside)].set(high)


def shard_levels(own_key, dims, cuts, low, high):
    gain = 1.0
    for position, blocks in cuts:
        steps = jax.random.uniform(jax.random.fold_in(jax.random.fold_in(own_key, 6), position), (blocks,), jnp.float32, low / len(cuts), high / len(cuts))
        gain = gain * jnp.repeat(jnp.exp(steps), dims[position] // blocks).reshape((-1,) + (1,) * (len(dims) - 1 - position))
    return gain


def assign_block(own_key, own, number, rows, number_of, top, bound, lean):
    sequence = jax.random.permutation(own_key, number_of)
    heavy_load, usual = shares(number_of, rows * top, bound, lean, True), shares(number_of, rows * top, bound, lean, False)
    places = jnp.arange(number_of)

    def named(tallies, rotation):
        used = int((tallies > 0).sum())
        fixed = max(1, used // 4)
        passed = fixed + (places - fixed + rotation * (used - fixed)) % max(1, number_of - fixed)
        return jnp.zeros((number_of,), jnp.int32).at[sequence[jnp.where(places < fixed, places, passed)]].set(jnp.asarray(tallies, jnp.int32))

    tallies = jnp.where(number % 4 == 0, named(heavy_load, number // 4), named(usual, number - number // 4 - 1))
    mixed = jax.random.permutation(jax.random.fold_in(own, 3), number_of)
    giver, receiver = mixed[0:number_of // 2 * 2:2], mixed[1:number_of // 2 * 2:2]
    slack = jnp.minimum(tallies[giver] - 1, bound - tallies[receiver]) // 2
    slack = jnp.where((giver == sequence[0]) | (receiver == sequence[0]) | (tallies[receiver] == 0), 0, jnp.maximum(slack, 0))
    passed = jax.random.randint(jax.random.fold_in(own, 4), (number_of // 2,), 0, 1 << 20) % (slack + 1)
    tallies = tallies.at[giver].add(-passed).at[receiver].add(passed)
    labels = jnp.searchsorted(jnp.cumsum(tallies), jnp.arange(rows * top), side="right").astype(jnp.int32)
    grid = labels.reshape(top, rows).T
    grid = grid[jax.random.permutation(jax.random.fold_in(own, 1), rows)]
    rotation = jax.random.randint(jax.random.fold_in(own, 2), (rows, 1), 0, top)
    return jnp.take_along_axis(grid, (jnp.arange(top)[None, :] + rotation) % top, axis=1)


def shares(number_of, total, reach, slope, full):
    portions = [(1 << 20) // math.isqrt(standing ** slope) + 1 for standing in range(1, number_of + 1)]
    largest = reach if full else min(reach, max(-(-total // number_of), total * portions[0] // sum(portions)))
    least = 1 if total - largest >= number_of - 1 else 0
    given, surplus = [largest] + [least] * (number_of - 1), total - largest - least * (number_of - 1)
    while surplus > 0:
        candidates = [i for i in range(1, number_of) if given[i] < largest] or [i for i in range(1, number_of) if given[i] < reach]
        whole, left = sum([portions[i] for i in candidates]), surplus
        for i in candidates:
            addition = min(reach - given[i], max(1, left * portions[i] // whole), surplus)
            given[i] = given[i] + addition
            surplus = surplus - addition
    return np.array(given)


def scatter_about(rng, dims, scale, reach, shards=(), kind=jnp.bfloat16):
    drawn = jax.random.normal(rng, dims, jnp.float32) * scale
    if len(shards) > 0:
        drawn = shard_levels(rng, dims, shards, -0.22, 0.18) * drawn
    return jnp.clip(drawn, min=-reach, max=reach).astype(kind)


def setup_inputs(seed: int = 0) -> dict:
    key_list = jax.random.split(jax.random.key(seed), 9)
    coeffs = scatter_about(key_list[0], (DROPLETS, 2 * COEF), 1.0, 6.0, ((0, 32),))
    t_matrix = jnp.clip(jax.random.uniform(key_list[1], (DROPLETS, 2 * COEF), jnp.float32, -0.7, 0.7) * shard_levels(key_list[1], (DROPLETS, 2 * COEF), ((0, 32),), -0.4, 0.0), -0.7, 0.7)
    trans_table = draw_trans_table(jax.random.fold_in(key_list[8], 71), 0)
    pair_source = place_ends(jax.random.randint(key_list[3], (PAIRS,), 0, N_GROUP * DROP_DEV), jax.random.fold_in(key_list[3], 1), 0, (N_GROUP * DROP_DEV) - 1).astype(jnp.int32)
    pair_owner_keys = jax.random.split(jax.random.fold_in(key_list[4], 1), PAIRS // (BLK_DEV * PAIR_BLOCK))
    pair_owner_turns = jax.random.permutation(jax.random.fold_in(key_list[4], 3), PAIRS // (BLK_DEV * PAIR_BLOCK))
    pair_owner = jax.vmap(lambda own, number: assign_block(jax.random.fold_in(key_list[4], 2), own, number, BLK_DEV * PAIR_BLOCK, 3 * N_GROUP, 1, CAP, 2))(pair_owner_keys, pair_owner_turns).reshape((PAIRS, 1))
    pair_row = place_ends(jax.random.randint(key_list[5], (PAIRS,), 0, DROP_DEV), jax.random.fold_in(key_list[5], 1), 0, DROP_DEV - 1).astype(jnp.int32)
    block_matrix = place_ends(jax.random.randint(key_list[6], (BLOCKS,), 0, MATS), jax.random.fold_in(key_list[6], 1), 0, MATS - 1).astype(jnp.int32)
    block_live = draw_block_live(jax.random.fold_in(key_list[8], 71), 0)
    return {"coeffs": coeffs, "t_matrix": t_matrix, "trans_table": trans_table, "pair_source": pair_source, "pair_owner": pair_owner, "pair_row": pair_row, "block_matrix": block_matrix, "block_live": block_live}


def reference(coeffs, t_matrix, trans_table, pair_source, pair_owner, pair_row, block_matrix, block_live):
    device_total = N_CLUSTER * N_GROUP
    coef_width = 2 * COEF
    span_rows = N_GROUP * DROP_DEV
    pair_count = BLK_DEV * PAIR_BLOCK
    start_field = jnp.zeros((device_total * DROP_DEV, coef_width), jnp.float32)

    def one_device(device, near_field):
        device = jnp.asarray(device).astype(jnp.int32)
        first_pair = device * pair_count
        source_ids = lax.dynamic_slice_in_dim(pair_source, first_pair, pair_count)
        cluster_index = device // N_GROUP
        first_row = cluster_index * span_rows
        picked = jnp.take(coeffs, (first_row + source_ids).astype(jnp.int32), axis=0)
        picked = picked.reshape(BLK_DEV, PAIR_BLOCK, coef_width).astype(jnp.float32)
        matrix_ids = lax.dynamic_slice_in_dim(block_matrix, device * BLK_DEV, BLK_DEV)
        matrices = jnp.take(trans_table, matrix_ids, axis=0).astype(jnp.float32)
        translated = jnp.einsum("bpi,bij->bpj", picked, matrices)
        alive = jnp.arange(BLK_DEV, dtype=jnp.int32) < block_live[device]
        translated = jnp.where(alive[:, None, None], translated, 0.0).astype(jnp.bfloat16)
        translated = translated.reshape(pair_count, coef_width).astype(jnp.float32)
        slots = lax.dynamic_slice_in_dim(pair_owner[:, 0], first_pair, pair_count)
        owner_cluster = jnp.mod(cluster_index + slots // N_GROUP - 1, N_CLUSTER)
        owners = owner_cluster * N_GROUP + jnp.mod(slots, N_GROUP)
        target_rows = lax.dynamic_slice_in_dim(pair_row, first_pair, pair_count)
        targets = (owners * DROP_DEV + target_rows).astype(jnp.int32)
        return near_field.at[targets].add(translated)

    near_field = lax.fori_loop(0, device_total, one_device, start_field)
    real_in = near_field[:, :COEF]
    imag_in = near_field[:, COEF:]
    real_t = t_matrix[:, :COEF]
    imag_t = t_matrix[:, COEF:]
    scattered = jnp.concatenate([real_in * real_t - imag_in * imag_t, real_in * imag_t + imag_in * real_t], axis=1)
    return coeffs.astype(jnp.float32) - scattered
```

```python
import functools

import jax
import jax.numpy as jnp
from jax import lax
from jax.experimental import pallas as pl
from jax.experimental.pallas import tpu as pltpu
from jax.sharding import PartitionSpec as P

LANES = 128
CHUNK = 128
NONE = 2**31 - 1
VMEM_BYTES = 60 * 2**20


def from_behind(value, axis, steps):
    count = lax.axis_size(axis)
    pairs = [(source, (source + steps) % count) for source in range(count)]
    return lax.ppermute(value, axis, pairs)


def windows_kernel(lists, span, window_rows, *refs):
    count = len(refs) // 2
    sources, outs = refs[:count], refs[count:]
    keys = sources[0][...]
    lane = lax.broadcasted_iota(jnp.int32, (window_rows, LANES), 1)
    place = lax.broadcasted_iota(jnp.int32, (window_rows, LANES), 0) * LANES + lane

    def below(bound):
        return jnp.sum((keys < bound).astype(jnp.int32))

    starts = [below(k * span) for k in range(lists)] + [below(lists * span)]
    for k in range(lists):
        start, length = starts[k], starts[k + 1] - starts[k]
        row, shift = start // LANES, start % LANES
        for source, out in zip(sources, outs):
            first = source[pl.ds(row, window_rows), :]
            second = source[pl.ds(row + 1, window_rows), :]
            turn = (LANES - shift) % LANES
            taken = jnp.where(
                lane < LANES - shift, pltpu.roll(first, turn, 1), pltpu.roll(second, turn, 1)
            )
            out[k] = jnp.where(place < length, taken, -1)


def cut_windows(arrays, lists, span, window_rows):
    rows = arrays[0].shape[0] // LANES
    padded = [
        jnp.concatenate([a.reshape(rows, LANES), jnp.full((16, LANES), NONE, jnp.int32)])
        for a in arrays
    ]
    shape = jax.ShapeDtypeStruct((lists, window_rows, LANES), jnp.int32)
    return pl.pallas_call(
        functools.partial(windows_kernel, lists, span, window_rows),
        out_shape=[shape] * len(arrays),
        in_specs=[pl.BlockSpec(memory_space=pltpu.VMEM)] * len(arrays),
        out_specs=[pl.BlockSpec(memory_space=pltpu.VMEM)] * len(arrays),
    )(*padded)


def field_kernel(
    phases, targets, mats,
    bounds, sources, rows, coeffs, table, out,
    wide, gather_a, gather_b, matrices, chunk_start, chunk_size, chunk_matrix, sems,
):
    coef_width = out.shape[2]
    parts = gather_a.shape[0] // CHUNK
    padded_width = parts * LANES
    entries = sources.shape[0] - CHUNK

    def fetch(m):
        return pltpu.make_async_copy(
            table.at[m], matrices.at[m, pl.ds(0, coef_width), :], sems.at[m]
        )

    def start_fetch(m, carry):
        matrices[m, pl.ds(coef_width, padded_width - coef_width), :] = jnp.zeros(
            (padded_width - coef_width, coef_width), jnp.bfloat16
        )
        fetch(m).start()
        return carry

    lax.fori_loop(0, mats, start_fetch, 0)

    def widen(i, carry):
        place = pl.multiple_of(i * 256, 256)
        wide[pl.ds(place, 256), :] = coeffs[pl.ds(place, 256), :].astype(jnp.float32)
        return carry

    lax.fori_loop(0, wide.shape[0] // 256, widen, 0)

    views = [sources.at[pl.ds(u, entries)] for u in range(CHUNK)]

    def gather(start, into):
        for u in range(CHUNK):
            place = pl.multiple_of(views[u][start], parts)
            into[pl.ds(u * parts, parts), :] = wide[pl.ds(place, parts), :]

    def picked(ref):
        return jnp.concatenate(
            [ref[pl.ds(k, CHUNK, stride=parts), :].astype(jnp.bfloat16) for k in range(parts)],
            axis=1,
        )

    lane = lax.broadcasted_iota(jnp.int32, (8, LANES), 1)
    target = lax.broadcasted_iota(jnp.int32, (targets, LANES), 0)

    def chosen(start, size):
        row, shift = start // LANES, start % LANES
        first = jnp.broadcast_to(rows[pl.ds(row, 1), :], (8, LANES))
        second = jnp.broadcast_to(rows[pl.ds(row + 1, 1), :], (8, LANES))
        turn = (LANES - shift) % LANES
        taken = jnp.where(
            lane < LANES - shift, pltpu.roll(first, turn, 1), pltpu.roll(second, turn, 1)
        )
        taken = jnp.where(lane < size, taken, -1)
        return (target == taken[:1]).astype(jnp.float32).astype(jnp.bfloat16)

    def translate(ref, m):
        return jnp.dot(picked(ref), matrices[m], preferred_element_type=jnp.float32).astype(
            jnp.bfloat16
        )

    fetched = 0
    for slot, phase in enumerate(phases):

        def list_chunks(m, j):
            start = bounds[phase * mats + m]
            length = bounds[phase * mats + m + 1] - start

            def put(i, carry):
                chunk_start[j + i] = start + i * CHUNK
                chunk_size[j + i] = jnp.minimum(length - i * CHUNK, CHUNK)
                chunk_matrix[j + i] = m
                return carry

            count = (length + CHUNK - 1) // CHUNK
            lax.fori_loop(0, count, put, 0)
            return j + count

        chunks = lax.fori_loop(0, mats, list_chunks, 0)
        for i in range(4):
            chunk_start[chunks + i] = 0
            chunk_size[chunks + i] = 0
            chunk_matrix[chunks + i] = 0
        out[slot] = jnp.zeros((targets, coef_width), jnp.float32)
        gather(chunk_start[0], gather_a)
        gather(chunk_start[1], gather_b)

        def step(i, fetched):
            j = 2 * i
            matrix_a, matrix_b = chunk_matrix[j], chunk_matrix[j + 1]
            needed = jnp.maximum(jnp.maximum(matrix_a, matrix_b) + 1, fetched)

            def await_one(m, carry):
                fetch(m).wait()
                return carry

            lax.fori_loop(fetched, needed, await_one, 0)
            lhs_a, lhs_b = picked(gather_a), picked(gather_b)
            start_a, start_b = chunk_start[j + 2], chunk_start[j + 3]
            gather(start_a, gather_a)
            gather(start_b, gather_b)
            record_a = jnp.dot(lhs_a, matrices[matrix_a], preferred_element_type=jnp.float32)
            record_b = jnp.dot(lhs_b, matrices[matrix_b], preferred_element_type=jnp.float32)
            records = jnp.concatenate(
                [record_a.astype(jnp.bfloat16), record_b.astype(jnp.bfloat16)], axis=0
            )
            places = jnp.concatenate(
                [
                    chosen(chunk_start[j], chunk_size[j]),
                    chosen(chunk_start[j + 1], chunk_size[j + 1]),
                ],
                axis=1,
            )
            out[slot] += jnp.dot(places, records, preferred_element_type=jnp.float32)
            return needed

        fetched = lax.fori_loop(0, (chunks + 1) // 2, step, fetched)

    def await_rest(m, carry):
        fetch(m).wait()
        return carry

    lax.fori_loop(fetched, mats, await_rest, 0)


def near_field(phases, targets, bounds, sources, rows, coeffs, table):
    mats, coef_width, _ = table.shape
    parts = -(-coef_width // LANES)
    most = sources.shape[0] // CHUNK + mats + 8
    return pl.pallas_call(
        functools.partial(field_kernel, phases, targets, mats),
        out_shape=jax.ShapeDtypeStruct((len(phases), targets, coef_width), jnp.float32),
        in_specs=[
            pl.BlockSpec(memory_space=pltpu.SMEM),
            pl.BlockSpec(memory_space=pltpu.SMEM),
            pl.BlockSpec(memory_space=pltpu.VMEM),
            pl.BlockSpec(memory_space=pltpu.VMEM),
            pl.BlockSpec(memory_space=pl.ANY),
        ],
        out_specs=pl.BlockSpec(memory_space=pltpu.VMEM),
        scratch_shapes=[
            pltpu.VMEM(coeffs.shape, jnp.float32),
            pltpu.VMEM((CHUNK * parts, LANES), jnp.float32),
            pltpu.VMEM((CHUNK * parts, LANES), jnp.float32),
            pltpu.VMEM((mats, parts * LANES, coef_width), jnp.bfloat16),
            pltpu.SMEM((most,), jnp.int32),
            pltpu.SMEM((most,), jnp.int32),
            pltpu.SMEM((most,), jnp.int32),
            pltpu.SemaphoreType.DMA((mats,)),
        ],
        compiler_params=pltpu.CompilerParams(vmem_limit_bytes=VMEM_BYTES),
    )(bounds, sources, rows, coeffs, table)


def on_device(
    coeffs, t_matrix, trans_table, pair_source, pair_owner, pair_row, block_matrix, block_live
):
    row_count, coef_width = coeffs.shape
    half_width = coef_width // 2
    mats = trans_table.shape[0]
    block_count = block_matrix.shape[0]
    pair_count = pair_source.shape[0]
    block_size = pair_count // block_count
    group_size = lax.axis_size("group")
    source_count = group_size * row_count
    lists = 3 * group_size
    capacity = pair_count // (2 * group_size)
    window_rows = -(-capacity // LANES)
    parts = -(-coef_width // LANES)

    padded = jnp.pad(coeffs, ((0, 0), (0, parts * LANES - coef_width)))
    cluster_rows = lax.all_gather(
        padded.reshape(row_count * parts, LANES), "group", axis=0, tiled=True
    )

    shape = (block_count, block_size)
    alive = jnp.arange(block_count, dtype=jnp.int32)[:, None] < block_live[0]
    owner = pair_owner[:, 0].reshape(shape)
    source, row = pair_source.reshape(shape), pair_row.reshape(shape)
    matrix = jnp.broadcast_to(block_matrix[:, None], shape)
    small = row * source_count + source
    small_span = row_count * source_count
    large = owner * mats + matrix
    if lists * mats * small_span < NONE:
        span = mats * small_span
        key = jnp.where(alive, large * small_span + small, NONE).reshape(-1)
        (window,) = cut_windows([lax.sort(key, is_stable=False)], lists, span, window_rows)
        valid = window >= 0
        matrix, small = window // small_span % mats, window % small_span
    else:
        key = jnp.where(alive, large, NONE).reshape(-1)
        ordered = lax.sort((key, small.reshape(-1)), num_keys=1, is_stable=False)
        window, small = cut_windows(list(ordered), lists, mats, window_rows)
        valid = window >= 0
        matrix = window % mats
    row, source = small // source_count, small % source_count
    fields = jnp.stack([jnp.where(valid, matrix, -1), row, source], axis=1).astype(jnp.int16)
    fields = fields.reshape(3, group_size, 3 * window_rows * LANES)
    fields = lax.all_to_all(fields, "group", split_axis=1, concat_axis=1, tiled=True)
    fields = fields.reshape(3, group_size, 3, window_rows * LANES).astype(jnp.int32)
    matrix, row, source = fields[:, :, 0], fields[:, :, 1], fields[:, :, 2]

    phase = jnp.arange(3, dtype=jnp.int32)[:, None, None]
    group_span = row_count * source_count
    key = (phase * mats + matrix) * group_span + row * source_count + source
    key = lax.sort(jnp.where(matrix >= 0, key, NONE).reshape(-1), is_stable=False)
    marks = jnp.arange(3 * mats + 1, dtype=jnp.int32) * group_span
    bounds = jnp.sum((key[None, :] < marks[:, None]).astype(jnp.int32), axis=1)
    places = key % source_count * parts
    rows = (key // source_count % row_count).reshape(-1, LANES)

    ahead = near_field((0, 2), row_count, bounds, places, rows, cluster_rows, trans_table)
    arrived = [from_behind(ahead[0], "cluster", -1), from_behind(ahead[1], "cluster", 1)]
    own = near_field((1,), row_count, bounds, places, rows, cluster_rows, trans_table)
    incoming = own[0] + arrived[0] + arrived[1]

    real_in, imag_in = incoming[:, :half_width], incoming[:, half_width:]
    real_t, imag_t = t_matrix[:, :half_width], t_matrix[:, half_width:]
    scattered = jnp.concatenate(
        [real_in * real_t - imag_in * imag_t, real_in * imag_t + imag_in * real_t], axis=1
    )
    return coeffs.astype(jnp.float32) - scattered


def solution(mesh):
    owned = P(("cluster", "group"))
    return jax.shard_map(
        on_device,
        mesh=mesh,
        in_specs=(owned, owned, P(), owned, owned, owned, owned, owned),
        out_specs=owned,
        check_vma=False,
    )
```

```python
import functools

import jax
import jax.numpy as jnp
from jax import lax
from jax.experimental import pallas as pl
from jax.experimental.pallas import tpu as pltpu
from jax.sharding import PartitionSpec as P

LANES = 128
SUBLANES = 8
ROWS = 16
UNIT = 256
SPAN = 512
PHASES = 6
EDGE_BITS = 5
EDGE = 2**EDGE_BITS - 1
PLACE_BITS = 2 * EDGE_BITS
NONE = 2**31 - 1
VMEM_BYTES = 60 * 2**20


def from_behind(value, axis, steps):
    count = lax.axis_size(axis)
    pairs = [(source, (source + steps) % count) for source in range(count)]
    return lax.ppermute(value, axis, pairs)


def digits(value, span):
    if span & (span - 1) == 0:
        return value >> (span.bit_length() - 1), value & (span - 1)
    return value // span, value % span


def ascending(tiles):
    tiles = list(tiles)
    count = len(tiles)
    low_bits = count.bit_length() - 1
    lane_bit = low_bits + 3
    total_bits = lane_bit + 7
    sublane = lax.broadcasted_iota(jnp.int32, (SUBLANES, LANES), 0)
    lane = lax.broadcasted_iota(jnp.int32, (SUBLANES, LANES), 1)

    def bit(i):
        return (sublane >> (i - low_bits) if i < lane_bit else lane >> (i - lane_bit)) & 1

    held = None
    for level in range(1, total_bits + 1):
        turned = [0] * count
        spread = None
        for at in (held, level):
            if at is None or at >= total_bits:
                continue
            if at < low_bits:
                turned = [turned[t] ^ (t >> at & 1) for t in range(count)]
            else:
                spread = bit(at) if spread is None else spread ^ bit(at)
        for t in range(count):
            if spread is not None:
                tiles[t] = tiles[t] ^ (~(-spread) if turned[t] else -spread)
            elif turned[t]:
                tiles[t] = ~tiles[t]
        held = level
        for j in range(level - 1, -1, -1):
            if j < low_bits:
                for t in range(count):
                    if not t >> j & 1:
                        u = t | 1 << j
                        tiles[t], tiles[u] = (
                            jnp.minimum(tiles[t], tiles[u]),
                            jnp.maximum(tiles[t], tiles[u]),
                        )
                continue
            axis, length, step = (
                (0, SUBLANES, 1 << (j - low_bits))
                if j < lane_bit
                else (1, LANES, 1 << (j - lane_bit))
            )
            low = bit(j) == 0
            for t in range(count):
                other = jnp.where(
                    low, pltpu.roll(tiles[t], length - step, axis), pltpu.roll(tiles[t], step, axis)
                )
                tiles[t] = jnp.where(
                    low, jnp.minimum(tiles[t], other), jnp.maximum(tiles[t], other)
                )
    return tiles


def in_order(tiles, scratch):
    count = len(tiles)
    for t in range(count):
        scratch[pl.ds(t * SUBLANES, SUBLANES), :] = tiles[t]
    whole = jnp.concatenate(
        [scratch[pl.ds(s, count, stride=SUBLANES), :] for s in range(SUBLANES)], axis=0
    )
    return [whole[i * LANES : (i + 1) * LANES].T for i in range(count * SUBLANES // LANES)]


def tiles_for(entries):
    tiles = 16
    while tiles * SUBLANES * LANES < entries:
        tiles *= 2
    return tiles


def cut_windows(group_size, mats, row_count, source_count, window_rows, fused, refs, out):
    keys = refs[0][...]
    small_span = row_count * source_count
    span = mats * small_span if fused else mats
    lane = lax.broadcasted_iota(jnp.int32, (window_rows, LANES), 1)
    place = lax.broadcasted_iota(jnp.int32, (window_rows, LANES), 0) * LANES + lane
    lists = 3 * group_size
    starts = [jnp.sum((keys < k * span).astype(jnp.int32)) for k in range(lists + 1)]
    for k in range(lists):
        length = starts[k + 1] - starts[k]
        front = digits(length + 1, 2)[0]
        for half, (start, size) in enumerate(
            ((starts[k], front), (starts[k] + front, length - front))
        ):
            row, shift = digits(start, LANES)
            turn = digits(LANES - shift, LANES)[1]

            def taken(ref):
                first = ref[pl.ds(row, window_rows), :]
                second = ref[pl.ds(row + 1, window_rows), :]
                return jnp.where(
                    lane < LANES - shift, pltpu.roll(first, turn, 1), pltpu.roll(second, turn, 1)
                )

            if fused:
                large, small = digits(taken(refs[0]), small_span)
            else:
                large, small = taken(refs[0]), taken(refs[1])
            matrix = jnp.where(place < size, digits(large, mats)[1], -1)
            offset, member = k // group_size, k % group_size
            to = (member // 2 * 2 + half) * 3 + offset
            held = pl.ds(member % 2 * window_rows, window_rows)
            for field, value in enumerate((matrix, *digits(small, source_count))):
                out[to, field, held, :] = value


def sort_and_cut_kernel(
    sizes, window_rows, live, block_matrix, owner, row, source, out, scratch, ordered
):
    group_size, mats, row_count, source_count = sizes
    blocks = owner.shape[0]
    sublane = lax.broadcasted_iota(jnp.int32, (SUBLANES, LANES), 0)
    tiles = []
    for t in range(scratch.shape[0] // SUBLANES):
        if t * SUBLANES >= blocks:
            tiles.append(jnp.full((SUBLANES, LANES), NONE, jnp.int32))
            continue
        held = pl.ds(t * SUBLANES, SUBLANES)
        matrix = jnp.zeros((SUBLANES, LANES), jnp.int32)
        for s in range(SUBLANES):
            matrix = jnp.where(sublane == s, block_matrix[t * SUBLANES + s], matrix)
        key = (owner[held, :] * mats + matrix) * row_count + row[held, :]
        key = key * source_count + source[held, :]
        tiles.append(jnp.where(sublane + t * SUBLANES < live[0], key, NONE))
    (ordered[...],) = in_order(ascending(tiles), scratch)
    cut_windows(group_size, mats, row_count, source_count, window_rows, True, [ordered], out)


def cut_kernel(sizes, window_rows, *refs):
    group_size, mats, row_count, source_count = sizes
    cut_windows(
        group_size, mats, row_count, source_count, window_rows, False, refs[:-1], refs[-1]
    )


def split_by_owner(sizes, window_rows, live, block_matrix, owner, row, source):
    group_size, mats, row_count, source_count = sizes
    smem, vmem = pl.BlockSpec(memory_space=pltpu.SMEM), pl.BlockSpec(memory_space=pltpu.VMEM)
    out = jax.ShapeDtypeStruct((3 * group_size, 3, 2 * window_rows, LANES), jnp.int32)
    lists = 3 * group_size
    tiles = tiles_for(owner.size)
    if lists * mats * row_count * source_count < NONE and tiles == LANES // SUBLANES:
        return pl.pallas_call(
            functools.partial(sort_and_cut_kernel, sizes, window_rows),
            out_shape=out,
            in_specs=[smem, smem, vmem, vmem, vmem],
            out_specs=vmem,
            scratch_shapes=[pltpu.VMEM((tiles * SUBLANES, LANES), jnp.int32)] * 2,
        )(live, block_matrix, owner, row, source)
    alive = jnp.arange(owner.shape[0], dtype=jnp.int32)[:, None] < live[0]
    large = jnp.where(alive, owner * mats + block_matrix[:, None], NONE).reshape(-1)
    small = (row * source_count + source).reshape(-1)
    held = [
        jnp.pad(a.reshape(-1, LANES), ((0, 16), (0, 0)), constant_values=NONE)
        for a in lax.sort((large, small), num_keys=1, is_stable=False)
    ]
    return pl.pallas_call(
        functools.partial(cut_kernel, sizes, window_rows),
        out_shape=out,
        in_specs=[vmem, vmem],
        out_specs=vmem,
    )(*held)


def plan(bounds, mats, trash, unit_blocks, shape, names_shape):
    def numbers(shape):
        return lax.broadcasted_iota(jnp.int32, shape, 0) * LANES + lax.broadcasted_iota(
            jnp.int32, shape, 1
        )

    block, number = numbers(shape), numbers(names_shape)
    whole_block = ROWS << PLACE_BITS

    def one_matrix(m, carry):
        unit, codes, names = carry
        j = unit * unit_blocks
        for p in range(PHASES):
            start, end = bounds[p * mats + m], bounds[p * mats + m + 1]
            first = digits(start, ROWS)[0]
            count = jnp.where(end > start, digits(end + ROWS - 1, ROWS)[0] - first, 0)
            code = block * whole_block + ((first - j) * whole_block + ROWS)
            code = jnp.where(block == j, code + (start - first * ROWS << EDGE_BITS), code)
            code = jnp.where(block == j + count - 1, code + (end - (first + count) * ROWS), code)
            codes = jnp.where((block >= j) & (block < j + count), code, codes)
            j = j + count
        last = digits(j + unit_blocks - 1, unit_blocks)[0]
        names = jnp.where((number >= unit) & (last > unit), m, names)
        return last, codes, names

    return lax.fori_loop(
        0,
        mats,
        one_matrix,
        (
            0,
            jnp.full(shape, (trash << PLACE_BITS) + ROWS, jnp.int32),
            jnp.zeros(names_shape, jnp.int32),
        ),
    )


def order_kernel(
    parts, row_count, source_count, mats, trash,
    bounds, keys, places, rows, codes, names, units, scratch,
):
    count = scratch.shape[0] // SUBLANES
    given = keys.shape[0] // SUBLANES
    tiles = [
        keys[pl.ds(t * SUBLANES, SUBLANES), :]
        if t < given
        else jnp.full((SUBLANES, LANES), NONE, jnp.int32)
        for t in range(count)
    ]
    strips = in_order(ascending(tiles), scratch)
    kept = places.shape[0] // len(strips)
    for i, strip in enumerate(strips):
        high, source = digits(strip[:kept], source_count)
        held = pl.ds(i, kept, stride=len(strips))
        places[held, :] = source * parts
        rows[held, :] = digits(high, row_count)[1]
    units[0], codes[...], names[...] = plan(
        bounds, mats, trash, UNIT // ROWS, codes.shape, names.shape
    )


def order_pairs(bounds, keys, parts, row_count, source_count, mats, most_pairs):
    tiles = tiles_for(keys.size)
    trash = -(-most_pairs // SPAN) * SPAN
    kept = (trash + SPAN) // LANES
    unit_blocks = UNIT // ROWS
    most_units = -(-(-(-most_pairs // ROWS) + 2 * PHASES * mats) // unit_blocks) + mats + 2
    tile = SUBLANES * LANES
    blocks = (-(-most_units * unit_blocks // tile) * SUBLANES, LANES)
    names = (-(-most_units // tile) * SUBLANES, LANES)
    smem, vmem = pl.BlockSpec(memory_space=pltpu.SMEM), pl.BlockSpec(memory_space=pltpu.VMEM)
    shapes = [(kept, LANES), (kept, LANES), blocks, names, (1,)]
    return pl.pallas_call(
        functools.partial(order_kernel, parts, row_count, source_count, mats, trash),
        out_shape=[jax.ShapeDtypeStruct(shape, jnp.int32) for shape in shapes],
        in_specs=[smem, vmem],
        out_specs=[vmem] * 4 + [smem],
        scratch_shapes=[pltpu.VMEM((tiles * SUBLANES, LANES), jnp.int32)],
    )(bounds, keys)


def field_kernel(
    targets, mats,
    bounds, codes, unit_matrix, all_units, sources, rows, coeffs, table, mine, theirs,
    wide, staged, gather_a, gather_b, matrices, records, total_ref, staged_sems, sems,
):
    coef_width = table.shape[2]
    units = all_units[0]
    parts = gather_a.shape[0] // UNIT
    padded_width = parts * LANES
    unit_blocks = UNIT // ROWS
    entries = sources.shape[0] - ROWS

    length = staged.shape[1]
    stretches = wide.shape[0] // length
    slots = staged.shape[0]

    def stage(i):
        return pltpu.make_async_copy(
            coeffs.at[pl.ds(i * length, length), :], staged.at[i % slots], staged_sems.at[i % slots]
        )

    for i in range(min(slots, stretches)):
        stage(i).start()

    def fetch(m):
        return pltpu.make_async_copy(
            table.at[m], matrices.at[m, pl.ds(0, coef_width), :], sems.at[m]
        )

    def start_fetch(m, carry):
        matrices[m, pl.ds(coef_width, padded_width - coef_width), :] = jnp.zeros(
            (padded_width - coef_width, coef_width), jnp.bfloat16
        )
        fetch(m).start()
        return carry

    first_used = unit_matrix[0]
    past_used = jnp.where(units > 0, unit_matrix[jnp.maximum(units, 1) - 1] + 1, first_used)
    lax.fori_loop(first_used, past_used, start_fetch, 0)

    for end in (bounds[0], bounds[PHASES * mats]):

        def clear(i, carry):
            place = pl.multiple_of(i * ROWS, ROWS)
            records[pl.ds(place, ROWS), :] = jnp.zeros((ROWS, coef_width), jnp.bfloat16)
            return carry

        span = digits(end, SPAN)[0]
        lax.fori_loop(span * (SPAN // ROWS), (span + 1) * (SPAN // ROWS), clear, 0)

    for i in range(stretches):
        stage(i).wait()

        def widen(j, carry, i=i):
            place = pl.multiple_of(j * 256, 256)
            wide[pl.ds(i * length + place, 256), :] = staged[i % slots, pl.ds(place, 256), :].astype(
                jnp.float32
            )
            return carry

        lax.fori_loop(0, length // 256, widen, 0)
        if i + slots < stretches:
            stage(i + slots).start()

    views = [sources.at[pl.ds(u, entries)] for u in range(ROWS)]
    row_of = lax.broadcasted_iota(jnp.int32, (ROWS, coef_width), 0)

    def gather(unit, into):
        for b in range(unit_blocks):
            start = codes[unit * unit_blocks + b] >> PLACE_BITS
            for u in range(ROWS):
                place = pl.multiple_of(views[u][start], parts)
                into[pl.ds((b * ROWS + u) * parts, parts), :] = wide[pl.ds(place, parts), :]

    def picked(ref):
        return jnp.concatenate(
            [ref[pl.ds(k, UNIT, stride=parts), :].astype(jnp.bfloat16) for k in range(parts)],
            axis=1,
        )

    def work(unit, held, coming):
        lhs = picked(held)
        gather(unit + 1, coming)
        product = jnp.dot(
            lhs, matrices[unit_matrix[unit]], preferred_element_type=jnp.float32
        ).astype(jnp.bfloat16)
        for b in range(unit_blocks):
            code = codes[unit * unit_blocks + b]
            place = pl.multiple_of(code >> PLACE_BITS, ROWS)
            low, high = code >> EDGE_BITS & EDGE, code & EDGE
            made = (row_of >= low) & (row_of < high)
            records[pl.ds(place, ROWS), :] = jnp.where(
                made, product[b * ROWS : (b + 1) * ROWS], records[pl.ds(place, ROWS), :]
            )

    gather(0, gather_a)

    def step(i, fetched):
        needed = jnp.maximum(jnp.maximum(unit_matrix[2 * i], unit_matrix[2 * i + 1]) + 1, fetched)

        def await_one(m, carry):
            fetch(m).wait()
            return carry

        lax.fori_loop(fetched, needed, await_one, 0)
        work(2 * i, gather_a, gather_b)
        work(2 * i + 1, gather_b, gather_a)
        return needed

    fetched = lax.fori_loop(0, digits(units + 1, 2)[0], step, first_used)

    def await_rest(m, carry):
        fetch(m).wait()
        return carry

    lax.fori_loop(fetched, past_used, await_rest, 0)

    target = lax.broadcasted_iota(jnp.int32, (targets, LANES), 0)
    lane = lax.broadcasted_iota(jnp.int32, (1, LANES), 1)

    for phase in range(PHASES):
        first, end = bounds[phase * mats], bounds[(phase + 1) * mats]

        def add_span(i, carry):
            places = []
            for k in range(SPAN // LANES):
                line = i * (SPAN // LANES) + k
                number = line * LANES + lane
                chosen = jnp.where(
                    (number >= first) & (number < end), rows[pl.ds(line, 1), :], -1
                )
                places.append((target == chosen).astype(jnp.float32).astype(jnp.bfloat16))
            held = records[pl.ds(pl.multiple_of(i * SPAN, SPAN), SPAN), :]
            total_ref[...] += jnp.dot(
                jnp.concatenate(places, axis=1), held, preferred_element_type=jnp.float32
            )
            return carry

        total_ref[...] = jnp.zeros((targets, coef_width), jnp.float32)
        lax.fori_loop(digits(first, SPAN)[0], digits(end + SPAN - 1, SPAN)[0], add_span, 0)
        if phase < mine.shape[0]:
            mine[phase, :, pl.ds(0, coef_width)] = total_ref[...]
        else:
            theirs[phase - mine.shape[0], :, pl.ds(0, coef_width)] = total_ref[...].astype(
                jnp.bfloat16
            )
    mine[:, :, pl.ds(coef_width, padded_width - coef_width)] = jnp.zeros(
        (mine.shape[0], targets, padded_width - coef_width), jnp.float32
    )
    theirs[:, :, pl.ds(coef_width, padded_width - coef_width)] = jnp.zeros(
        (mine.shape[0], targets, padded_width - coef_width), jnp.bfloat16
    )


def near_field(targets, bounds, codes, names, units, places, rows, coeffs, table):
    mats, coef_width, _ = table.shape
    parts = -(-coef_width // LANES)
    smem, vmem = pl.BlockSpec(memory_space=pltpu.SMEM), pl.BlockSpec(memory_space=pltpu.VMEM)
    shape = (PHASES // 2, targets, parts * LANES)
    return pl.pallas_call(
        functools.partial(field_kernel, targets, mats),
        out_shape=[
            jax.ShapeDtypeStruct(shape, jnp.float32),
            jax.ShapeDtypeStruct(shape, jnp.bfloat16),
        ],
        in_specs=[smem] * 5 + [vmem] + [pl.BlockSpec(memory_space=pl.ANY)] * 2,
        out_specs=[vmem] * 2,
        scratch_shapes=[
            pltpu.VMEM(coeffs.shape, jnp.float32),
            pltpu.VMEM((4, 2048, LANES), jnp.bfloat16),
            pltpu.VMEM((UNIT * parts, LANES), jnp.float32),
            pltpu.VMEM((UNIT * parts, LANES), jnp.float32),
            pltpu.VMEM((mats, parts * LANES, coef_width), jnp.bfloat16),
            pltpu.VMEM((rows.size, coef_width), jnp.bfloat16),
            pltpu.VMEM((targets, coef_width), jnp.float32),
            pltpu.SemaphoreType.DMA((4,)),
            pltpu.SemaphoreType.DMA((mats,)),
        ],
        compiler_params=pltpu.CompilerParams(vmem_limit_bytes=VMEM_BYTES),
    )(
        bounds, codes.reshape(-1), names.reshape(-1), units,
        places.reshape(-1), rows, coeffs, table,
    )


def on_device(
    coeffs, t_matrix, trans_table, pair_source, pair_owner, pair_row, block_matrix, block_live
):
    row_count, coef_width = coeffs.shape
    half_width = coef_width // 2
    mats = trans_table.shape[0]
    block_count = block_matrix.shape[0]
    pair_count = pair_source.shape[0]
    group_size = lax.axis_size("group")
    source_count = group_size * row_count
    capacity = pair_count // (2 * group_size)
    most_pairs = 3 * group_size * capacity
    window_rows = -(-((capacity + 1) // 2) // LANES)
    parts = -(-coef_width // LANES)

    padded = jnp.pad(coeffs, ((0, 0), (0, parts * LANES - coef_width)))
    cluster_rows = lax.all_gather(
        padded.reshape(row_count * parts, LANES), "group", axis=0, tiled=True
    )

    shape = (block_count, pair_count // block_count)
    fields = split_by_owner(
        (group_size, mats, row_count, source_count),
        window_rows,
        block_live,
        block_matrix,
        pair_owner.reshape(shape),
        pair_row.reshape(shape),
        pair_source.reshape(shape),
    )
    window = window_rows * LANES
    fields = fields.reshape(group_size, 3, 6 * window).astype(jnp.int16)
    fields = lax.all_to_all(fields, "group", split_axis=0, concat_axis=0, tiled=True)
    fields = fields.reshape(group_size, 3, 3, 2, window).astype(jnp.int32)
    matrix, row, source = fields[:, :, 0], fields[:, :, 1], fields[:, :, 2]

    member = lax.axis_index("group") % 2
    beside = jnp.arange(2, dtype=jnp.int32)[None, None, :, None] ^ member
    offset = jnp.arange(3, dtype=jnp.int32)[None, :, None, None]
    phase = 3 * beside + offset
    span = row_count * source_count
    key = (phase * mats + matrix) * span + row * source_count + source
    key = jnp.where(matrix >= 0, key, NONE)
    marks = jnp.arange(PHASES * mats + 1, dtype=jnp.int32) * span
    bounds = jnp.sum((key.reshape(1, -1) < marks[:, None]).astype(jnp.int32), axis=1)
    places, rows, codes, names, units = order_pairs(
        bounds, key.reshape(-1, LANES), parts, row_count, source_count, mats, most_pairs
    )
    mine, theirs = near_field(
        row_count, bounds, codes, names, units, places, rows, cluster_rows, trans_table
    )
    swap = [(g, g ^ 1) for g in range(group_size)]
    sums = mine + lax.ppermute(theirs, "group", swap).astype(jnp.float32)
    arrived = [
        from_behind(sums[0].astype(jnp.bfloat16), "cluster", -1),
        from_behind(sums[2].astype(jnp.bfloat16), "cluster", 1),
    ]
    incoming = sums[1] + arrived[0].astype(jnp.float32) + arrived[1].astype(jnp.float32)
    incoming = incoming[:, :coef_width]

    real_in, imag_in = incoming[:, :half_width], incoming[:, half_width:]
    real_t, imag_t = t_matrix[:, :half_width], t_matrix[:, half_width:]
    scattered = jnp.concatenate(
        [real_in * real_t - imag_in * imag_t, real_in * imag_t + imag_in * real_t], axis=1
    )
    return coeffs.astype(jnp.float32) - scattered


def solution(mesh):
    owned = P(("cluster", "group"))
    return jax.shard_map(
        on_device,
        mesh=mesh,
        in_specs=(owned, owned, P(), owned, owned, owned, owned, owned),
        out_specs=owned,
        check_vma=False,
    )
```

```python
import functools

import jax
import jax.numpy as jnp
from jax import lax
from jax.experimental import pallas as pl
from jax.experimental.pallas import tpu as pltpu
from jax.sharding import PartitionSpec as P

LANES = 128
SUBLANES = 8
ROWS = 16
UNIT = 256
SPAN = 512
PHASES = 6
EDGE_BITS = 5
EDGE = 2**EDGE_BITS - 1
PLACE_BITS = 2 * EDGE_BITS
NONE = 2**31 - 1
VMEM_BYTES = 60 * 2**20


def from_behind(value, axis, steps):
    count = lax.axis_size(axis)
    pairs = [(source, (source + steps) % count) for source in range(count)]
    return lax.ppermute(value, axis, pairs)


def digits(value, span):
    if span & (span - 1) == 0:
        return value >> (span.bit_length() - 1), value & (span - 1)
    return value // span, value % span


def ascending(tiles):
    tiles = list(tiles)
    count = len(tiles)
    low_bits = count.bit_length() - 1
    lane_bit = low_bits + 3
    total_bits = lane_bit + 7
    sublane = lax.broadcasted_iota(jnp.int32, (SUBLANES, LANES), 0)
    lane = lax.broadcasted_iota(jnp.int32, (SUBLANES, LANES), 1)

    def bit(i):
        return (sublane >> (i - low_bits) if i < lane_bit else lane >> (i - lane_bit)) & 1

    held = None
    for level in range(1, total_bits + 1):
        turned = [0] * count
        spread = None
        for at in (held, level):
            if at is None or at >= total_bits:
                continue
            if at < low_bits:
                turned = [turned[t] ^ (t >> at & 1) for t in range(count)]
            else:
                spread = bit(at) if spread is None else spread ^ bit(at)
        for t in range(count):
            if spread is not None:
                tiles[t] = tiles[t] ^ (~(-spread) if turned[t] else -spread)
            elif turned[t]:
                tiles[t] = ~tiles[t]
        held = level
        for j in range(level - 1, -1, -1):
            if j < low_bits:
                for t in range(count):
                    if not t >> j & 1:
                        u = t | 1 << j
                        tiles[t], tiles[u] = (
                            jnp.minimum(tiles[t], tiles[u]),
                            jnp.maximum(tiles[t], tiles[u]),
                        )
                continue
            axis, length, step = (
                (0, SUBLANES, 1 << (j - low_bits))
                if j < lane_bit
                else (1, LANES, 1 << (j - lane_bit))
            )
            low = bit(j) == 0
            for t in range(count):
                other = jnp.where(
                    low, pltpu.roll(tiles[t], length - step, axis), pltpu.roll(tiles[t], step, axis)
                )
                tiles[t] = jnp.where(
                    low, jnp.minimum(tiles[t], other), jnp.maximum(tiles[t], other)
                )
    return tiles


def in_order(tiles, scratch):
    count = len(tiles)
    for t in range(count):
        scratch[pl.ds(t * SUBLANES, SUBLANES), :] = tiles[t]
    whole = jnp.concatenate(
        [scratch[pl.ds(s, count, stride=SUBLANES), :] for s in range(SUBLANES)], axis=0
    )
    return [whole[i * LANES : (i + 1) * LANES].T for i in range(count * SUBLANES // LANES)]


def tiles_for(entries):
    tiles = 16
    while tiles * SUBLANES * LANES < entries:
        tiles *= 2
    return tiles


def cut_windows(group_size, mats, row_count, source_count, window_rows, fused, refs, sent, out):
    keys = refs[0][...]
    small_span = row_count * source_count
    span = mats * small_span if fused else mats
    lane = lax.broadcasted_iota(jnp.int32, (window_rows, LANES), 1)
    place = lax.broadcasted_iota(jnp.int32, (window_rows, LANES), 0) * LANES + lane
    lists = 3 * group_size
    starts = [jnp.sum((keys < k * span).astype(jnp.int32)) for k in range(lists + 1)]
    for k in range(lists):
        length = starts[k + 1] - starts[k]
        front = digits(length + 1, 2)[0]
        for half, (start, size) in enumerate(
            ((starts[k], front), (starts[k] + front, length - front))
        ):
            row, shift = digits(start, LANES)
            turn = digits(LANES - shift, LANES)[1]

            def taken(ref):
                first = ref[pl.ds(row, window_rows), :]
                second = ref[pl.ds(row + 1, window_rows), :]
                return jnp.where(
                    lane < LANES - shift, pltpu.roll(first, turn, 1), pltpu.roll(second, turn, 1)
                )

            if fused:
                large, small = digits(taken(refs[0]), small_span)
            else:
                large, small = taken(refs[0]), taken(refs[1])
            matrix = jnp.where(place < size, digits(large, mats)[1], -1)
            offset, member = k // group_size, k % group_size
            to = member // 2 * 2 + half
            first = ((to * 3 + offset) * 3 * 2 + member % 2) * window_rows
            first += to * (sent.shape[0] // group_size - 18 * window_rows)
            for field, value in enumerate((matrix, *digits(small, source_count))):
                sent[pl.ds(first + field * 2 * window_rows, window_rows), :] = value
    rows = 2 * ROWS
    for i in range(sent.shape[0] // rows):
        out[pl.ds(i * rows, rows), :] = sent[pl.ds(i * rows, rows), :].astype(jnp.int16)


def sort_and_cut_kernel(
    sizes, window_rows, live, block_matrix, owner, row, source, out, sent, scratch, ordered
):
    group_size, mats, row_count, source_count = sizes
    blocks = owner.shape[0]
    sublane = lax.broadcasted_iota(jnp.int32, (SUBLANES, LANES), 0)
    tiles = []
    for t in range(scratch.shape[0] // SUBLANES):
        if t * SUBLANES >= blocks:
            tiles.append(jnp.full((SUBLANES, LANES), NONE, jnp.int32))
            continue
        held = pl.ds(t * SUBLANES, SUBLANES)
        matrix = jnp.zeros((SUBLANES, LANES), jnp.int32)
        for s in range(SUBLANES):
            matrix = jnp.where(sublane == s, block_matrix[t * SUBLANES + s], matrix)
        key = (owner[held, :] * mats + matrix) * row_count + row[held, :]
        key = key * source_count + source[held, :]
        tiles.append(jnp.where(sublane + t * SUBLANES < live[0], key, NONE))
    (ordered[...],) = in_order(ascending(tiles), scratch)
    cut_windows(group_size, mats, row_count, source_count, window_rows, True, [ordered], sent, out)


def cut_kernel(sizes, window_rows, *refs):
    group_size, mats, row_count, source_count = sizes
    cut_windows(
        group_size, mats, row_count, source_count, window_rows, False, refs[:2], refs[3], refs[2]
    )


def split_by_owner(sizes, window_rows, live, block_matrix, owner, row, source):
    group_size, mats, row_count, source_count = sizes
    smem, vmem = pl.BlockSpec(memory_space=pltpu.SMEM), pl.BlockSpec(memory_space=pltpu.VMEM)
    message = -(-18 * window_rows // (2 * ROWS)) * 2 * ROWS
    shape = (group_size * message, LANES)
    out = jax.ShapeDtypeStruct(shape, jnp.int16)
    lists = 3 * group_size
    tiles = tiles_for(owner.size)
    if lists * mats * row_count * source_count < NONE and tiles == LANES // SUBLANES:
        return pl.pallas_call(
            functools.partial(sort_and_cut_kernel, sizes, window_rows),
            out_shape=out,
            in_specs=[smem, smem, vmem, vmem, vmem],
            out_specs=vmem,
            scratch_shapes=[pltpu.VMEM(shape, jnp.int32)]
            + [pltpu.VMEM((tiles * SUBLANES, LANES), jnp.int32)] * 2,
        )(live, block_matrix, owner, row, source)
    alive = jnp.arange(owner.shape[0], dtype=jnp.int32)[:, None] < live[0]
    large = jnp.where(alive, owner * mats + block_matrix[:, None], NONE).reshape(-1)
    small = (row * source_count + source).reshape(-1)
    held = [
        jnp.pad(a.reshape(-1, LANES), ((0, 16), (0, 0)), constant_values=NONE)
        for a in lax.sort((large, small), num_keys=1, is_stable=False)
    ]
    return pl.pallas_call(
        functools.partial(cut_kernel, sizes, window_rows),
        out_shape=out,
        in_specs=[vmem, vmem],
        out_specs=vmem,
        scratch_shapes=[pltpu.VMEM(shape, jnp.int32)],
    )(*held)


def plan(bounds, mats, trash, unit_blocks, shape, names_shape):
    def numbers(shape):
        return lax.broadcasted_iota(jnp.int32, shape, 0) * LANES + lax.broadcasted_iota(
            jnp.int32, shape, 1
        )

    block, number = numbers(shape), numbers(names_shape)
    whole_block = ROWS << PLACE_BITS

    def one_matrix(m, carry):
        unit, codes, names = carry
        j = unit * unit_blocks
        for p in range(PHASES):
            start, end = bounds[p * mats + m], bounds[p * mats + m + 1]
            first = digits(start, ROWS)[0]
            count = jnp.where(end > start, digits(end + ROWS - 1, ROWS)[0] - first, 0)
            code = block * whole_block + ((first - j) * whole_block + ROWS)
            code = jnp.where(block == j, code + (start - first * ROWS << EDGE_BITS), code)
            code = jnp.where(block == j + count - 1, code + (end - (first + count) * ROWS), code)
            codes = jnp.where((block >= j) & (block < j + count), code, codes)
            j = j + count
        last = digits(j + unit_blocks - 1, unit_blocks)[0]
        names = jnp.where((number >= unit) & (last > unit), m, names)
        return last, codes, names

    return lax.fori_loop(
        0,
        mats,
        one_matrix,
        (
            0,
            jnp.full(shape, (trash << PLACE_BITS) + ROWS, jnp.int32),
            jnp.zeros(names_shape, jnp.int32),
        ),
    )


def order_kernel(
    parts, row_count, source_count, mats, trash,
    bounds, keys, places, rows, codes, names, units, scratch,
):
    count = scratch.shape[0] // SUBLANES
    given = keys.shape[0] // SUBLANES
    tiles = [
        keys[pl.ds(t * SUBLANES, SUBLANES), :]
        if t < given
        else jnp.full((SUBLANES, LANES), NONE, jnp.int32)
        for t in range(count)
    ]
    strips = in_order(ascending(tiles), scratch)
    kept = places.shape[0] // len(strips)
    for i, strip in enumerate(strips):
        high, source = digits(strip[:kept], source_count)
        held = pl.ds(i, kept, stride=len(strips))
        places[held, :] = source * parts
        rows[held, :] = digits(high, row_count)[1]
    units[0], codes[...], names[...] = plan(
        bounds, mats, trash, UNIT // ROWS, codes.shape, names.shape
    )


def order_pairs(bounds, keys, parts, row_count, source_count, mats, most_pairs):
    tiles = tiles_for(keys.size)
    trash = -(-most_pairs // SPAN) * SPAN
    kept = (trash + SPAN) // LANES
    unit_blocks = UNIT // ROWS
    most_units = -(-(-(-most_pairs // ROWS) + 2 * PHASES * mats) // unit_blocks) + mats + 6
    tile = SUBLANES * LANES
    blocks = (-(-most_units * unit_blocks // tile) * SUBLANES, LANES)
    names = (-(-most_units // tile) * SUBLANES, LANES)
    smem, vmem = pl.BlockSpec(memory_space=pltpu.SMEM), pl.BlockSpec(memory_space=pltpu.VMEM)
    shapes = [(kept, LANES), (kept, LANES), blocks, names, (1,)]
    return pl.pallas_call(
        functools.partial(order_kernel, parts, row_count, source_count, mats, trash),
        out_shape=[jax.ShapeDtypeStruct(shape, jnp.int32) for shape in shapes],
        in_specs=[smem, vmem],
        out_specs=[vmem] * 4 + [smem],
        scratch_shapes=[pltpu.VMEM((tiles * SUBLANES, LANES), jnp.int32)],
    )(bounds, keys)


def field_kernel(
    targets, mats,
    bounds, codes, unit_matrix, all_units, rows, places, coeffs, table, before, own, after, theirs,
    sources, wide, staged, gather_a, gather_b, gather_c, gather_d, matrices, records, total_ref, places_sem, staged_sems, sems,
):
    coef_width = table.shape[2]
    units = all_units[0]
    mine = (before, own, after)
    parts = gather_a.shape[0] // UNIT
    padded_width = parts * LANES
    unit_blocks = UNIT // ROWS
    entries = sources.shape[0] - ROWS

    length = staged.shape[1]
    stretches = wide.shape[0] // length
    slots = staged.shape[0]

    def stage(i):
        return pltpu.make_async_copy(
            coeffs.at[pl.ds(i * length, length), :], staged.at[i % slots], staged_sems.at[i % slots]
        )

    listing = pltpu.make_async_copy(places, sources, places_sem)
    listing.start()
    for i in range(min(slots, stretches)):
        stage(i).start()

    def fetch(m):
        return pltpu.make_async_copy(
            table.at[m], matrices.at[m, pl.ds(0, coef_width), :], sems.at[m]
        )

    def start_fetch(m, carry):
        matrices[m, pl.ds(coef_width, padded_width - coef_width), :] = jnp.zeros(
            (padded_width - coef_width, coef_width), jnp.bfloat16
        )
        fetch(m).start()
        return carry

    first_used = unit_matrix[0]
    past_used = jnp.where(units > 0, unit_matrix[jnp.maximum(units, 1) - 1] + 1, first_used)
    lax.fori_loop(first_used, past_used, start_fetch, 0)

    for end in (bounds[0], bounds[PHASES * mats]):

        def clear(i, carry):
            place = pl.multiple_of(i * ROWS, ROWS)
            records[pl.ds(place, ROWS), :] = jnp.zeros((ROWS, coef_width), jnp.bfloat16)
            return carry

        span = digits(end, SPAN)[0]
        lax.fori_loop(span * (SPAN // ROWS), (span + 1) * (SPAN // ROWS), clear, 0)

    for i in range(stretches):
        stage(i).wait()

        def widen(j, carry, i=i):
            place = pl.multiple_of(j * 256, 256)
            wide[pl.ds(i * length + place, 256), :] = staged[i % slots, pl.ds(place, 256), :].astype(
                jnp.float32
            )
            return carry

        lax.fori_loop(0, length // 256, widen, 0)
        if i + slots < stretches:
            stage(i + slots).start()

    views = [sources.at[pl.ds(u, entries)] for u in range(ROWS)]
    row_of = lax.broadcasted_iota(jnp.int32, (ROWS, coef_width), 0)

    def gather(unit, into):
        for b in range(unit_blocks):
            start = codes[unit * unit_blocks + b] >> PLACE_BITS
            for u in range(ROWS):
                place = pl.multiple_of(views[u][start], parts)
                into[pl.ds((b * ROWS + u) * parts, parts), :] = wide[pl.ds(place, parts), :]

    def picked(ref):
        return jnp.concatenate(
            [ref[pl.ds(k, UNIT, stride=parts), :].astype(jnp.bfloat16) for k in range(parts)],
            axis=1,
        )

    def work(unit, held, coming):
        lhs = picked(held)
        gather(unit + 2, coming)
        product = jnp.dot(
            lhs, matrices[unit_matrix[unit]], preferred_element_type=jnp.float32
        ).astype(jnp.bfloat16)
        for b in range(unit_blocks):
            code = codes[unit * unit_blocks + b]
            place = pl.multiple_of(code >> PLACE_BITS, ROWS)
            low, high = code >> EDGE_BITS & EDGE, code & EDGE
            made = (row_of >= low) & (row_of < high)
            records[pl.ds(place, ROWS), :] = jnp.where(
                made, product[b * ROWS : (b + 1) * ROWS], records[pl.ds(place, ROWS), :]
            )

    listing.wait()
    gather(0, gather_a)
    gather(1, gather_b)

    def step(i, fetched):
        needed = jnp.maximum(
            jnp.maximum(
                jnp.maximum(unit_matrix[4 * i], unit_matrix[4 * i + 1]),
                jnp.maximum(unit_matrix[4 * i + 2], unit_matrix[4 * i + 3]),
            )
            + 1,
            fetched,
        )

        def await_one(m, carry):
            fetch(m).wait()
            return carry

        lax.fori_loop(fetched, needed, await_one, 0)
        work(4 * i, gather_a, gather_c)
        work(4 * i + 1, gather_b, gather_d)
        work(4 * i + 2, gather_c, gather_a)
        work(4 * i + 3, gather_d, gather_b)
        return needed

    fetched = lax.fori_loop(0, digits(units + 3, 4)[0], step, first_used)

    def await_rest(m, carry):
        fetch(m).wait()
        return carry

    lax.fori_loop(fetched, past_used, await_rest, 0)

    target = lax.broadcasted_iota(jnp.int32, (targets, LANES), 0)
    lane = lax.broadcasted_iota(jnp.int32, (1, LANES), 1)

    for phase in range(PHASES):
        first, end = bounds[phase * mats], bounds[(phase + 1) * mats]

        def add_span(i, carry):
            places = []
            for k in range(SPAN // LANES):
                line = i * (SPAN // LANES) + k
                number = line * LANES + lane
                chosen = jnp.where(
                    (number >= first) & (number < end), rows[pl.ds(line, 1), :], -1
                )
                places.append((target == chosen).astype(jnp.float32).astype(jnp.bfloat16))
            held = records[pl.ds(pl.multiple_of(i * SPAN, SPAN), SPAN), :]
            total_ref[...] += jnp.dot(
                jnp.concatenate(places, axis=1), held, preferred_element_type=jnp.float32
            )
            return carry

        total_ref[...] = jnp.zeros((targets, coef_width), jnp.float32)
        lax.fori_loop(digits(first, SPAN)[0], digits(end + SPAN - 1, SPAN)[0], add_span, 0)
        if phase < len(mine):
            mine[phase][:, pl.ds(0, coef_width)] = total_ref[...]
        else:
            theirs[phase - len(mine), :, pl.ds(0, coef_width)] = total_ref[...].astype(
                jnp.bfloat16
            )
    rest = padded_width - coef_width
    for out in mine:
        out[:, pl.ds(coef_width, rest)] = jnp.zeros((targets, rest), jnp.float32)
    theirs[:, :, pl.ds(coef_width, rest)] = jnp.zeros((len(mine), targets, rest), jnp.bfloat16)


def near_field(targets, bounds, codes, names, units, places, rows, coeffs, table):
    mats, coef_width, _ = table.shape
    parts = -(-coef_width // LANES)
    smem, vmem = pl.BlockSpec(memory_space=pltpu.SMEM), pl.BlockSpec(memory_space=pltpu.VMEM)
    shape = (targets, parts * LANES)
    return pl.pallas_call(
        functools.partial(field_kernel, targets, mats),
        out_shape=[jax.ShapeDtypeStruct(shape, jnp.float32)] * 3
        + [jax.ShapeDtypeStruct((3, *shape), jnp.bfloat16)],
        in_specs=[smem] * 4 + [vmem] + [pl.BlockSpec(memory_space=pl.ANY)] * 3,
        out_specs=[vmem] * 4,
        scratch_shapes=[
            pltpu.SMEM((places.size,), jnp.int32),
            pltpu.VMEM(coeffs.shape, jnp.float32),
            pltpu.VMEM((4, 2048, LANES), jnp.bfloat16),
            pltpu.VMEM((UNIT * parts, LANES), jnp.float32),
            pltpu.VMEM((UNIT * parts, LANES), jnp.float32),
            pltpu.VMEM((UNIT * parts, LANES), jnp.float32),
            pltpu.VMEM((UNIT * parts, LANES), jnp.float32),
            pltpu.VMEM((mats, parts * LANES, coef_width), jnp.bfloat16),
            pltpu.VMEM((rows.size, coef_width), jnp.bfloat16),
            pltpu.VMEM((targets, coef_width), jnp.float32),
            pltpu.SemaphoreType.DMA,
            pltpu.SemaphoreType.DMA((4,)),
            pltpu.SemaphoreType.DMA((mats,)),
        ],
        compiler_params=pltpu.CompilerParams(vmem_limit_bytes=VMEM_BYTES),
    )(
        bounds, codes.reshape(-1), names.reshape(-1), units, rows, places.reshape(-1), coeffs, table
    )


def on_device(
    coeffs, t_matrix, trans_table, pair_source, pair_owner, pair_row, block_matrix, block_live
):
    row_count, coef_width = coeffs.shape
    half_width = coef_width // 2
    mats = trans_table.shape[0]
    block_count = block_matrix.shape[0]
    pair_count = pair_source.shape[0]
    group_size = lax.axis_size("group")
    source_count = group_size * row_count
    capacity = pair_count // (2 * group_size)
    most_pairs = 3 * group_size * capacity
    window_rows = -(-((capacity + 1) // 2) // LANES)
    parts = -(-coef_width // LANES)

    padded = jnp.pad(coeffs, ((0, 0), (0, parts * LANES - coef_width)))
    cluster_rows = lax.all_gather(
        padded.reshape(row_count * parts, LANES), "group", axis=0, tiled=True
    )

    shape = (block_count, pair_count // block_count)
    fields = split_by_owner(
        (group_size, mats, row_count, source_count),
        window_rows,
        block_live,
        block_matrix,
        pair_owner.reshape(shape),
        pair_row.reshape(shape),
        pair_source.reshape(shape),
    )
    window = window_rows * LANES
    fields = fields.reshape(group_size, -1, LANES)
    fields = lax.all_to_all(fields, "group", split_axis=0, concat_axis=0, tiled=True)
    fields = fields[:, : 18 * window_rows].reshape(group_size, 3, 3, 2, window).astype(jnp.int32)
    matrix, row, source = fields[:, :, 0], fields[:, :, 1], fields[:, :, 2]

    member = lax.axis_index("group") % 2
    beside = jnp.arange(2, dtype=jnp.int32)[None, None, :, None] ^ member
    offset = jnp.arange(3, dtype=jnp.int32)[None, :, None, None]
    phase = 3 * beside + offset
    span = row_count * source_count
    key = (phase * mats + matrix) * span + row * source_count + source
    key = jnp.where(matrix >= 0, key, NONE)
    marks = jnp.arange(PHASES * mats + 1, dtype=jnp.int32) * span
    bounds = jnp.sum((key.reshape(1, -1) < marks[:, None]).astype(jnp.int32), axis=1)
    places, rows, codes, names, units = order_pairs(
        bounds, key.reshape(-1, LANES), parts, row_count, source_count, mats, most_pairs
    )
    before, own, after, theirs = near_field(
        row_count, bounds, codes, names, units, places, rows, cluster_rows, trans_table
    )
    swap = [(g, g ^ 1) for g in range(group_size)]
    shared = lax.ppermute(theirs, "group", swap).astype(jnp.float32)
    from_after = from_behind((before + shared[0]).astype(jnp.bfloat16), "cluster", -1)
    from_before = from_behind((after + shared[2]).astype(jnp.bfloat16), "cluster", 1)
    incoming = own + shared[1] + from_after.astype(jnp.float32) + from_before.astype(jnp.float32)
    incoming = incoming[:, :coef_width]

    real_in, imag_in = incoming[:, :half_width], incoming[:, half_width:]
    real_t, imag_t = t_matrix[:, :half_width], t_matrix[:, half_width:]
    scattered = jnp.concatenate(
        [real_in * real_t - imag_in * imag_t, real_in * imag_t + imag_in * real_t], axis=1
    )
    return coeffs.astype(jnp.float32) - scattered


def solution(mesh):
    owned = P(("cluster", "group"))
    return jax.shard_map(
        on_device,
        mesh=mesh,
        in_specs=(owned, owned, P(), owned, owned, owned, owned, owned),
        out_specs=owned,
        check_vma=False,
    )
```

```python
import functools

import jax
import jax.numpy as jnp
from jax import lax
from jax.experimental import pallas as pl
from jax.experimental.pallas import tpu as pltpu
from jax.sharding import PartitionSpec as P

LANES = 128
SUBLANES = 8
ROWS = 16
UNIT = 256
SPAN = 512
STAGE = 512
WIDEN = 64
PHASES = 6
EDGE_BITS = 5
EDGE = 2**EDGE_BITS - 1
PLACE_BITS = 2 * EDGE_BITS
NONE = 2**31 - 1
VMEM_BYTES = 60 * 2**20


def from_behind(value, axis, steps):
    count = lax.axis_size(axis)
    pairs = [(source, (source + steps) % count) for source in range(count)]
    return lax.ppermute(value, axis, pairs)


def digits(value, span):
    if span & (span - 1) == 0:
        return value >> (span.bit_length() - 1), value & (span - 1)
    return value // span, value % span


def ascending(tiles):
    tiles = list(tiles)
    count = len(tiles)
    low_bits = count.bit_length() - 1
    lane_bit = low_bits + 3
    total_bits = lane_bit + 7
    sublane = lax.broadcasted_iota(jnp.int32, (SUBLANES, LANES), 0)
    lane = lax.broadcasted_iota(jnp.int32, (SUBLANES, LANES), 1)

    def bit(i):
        return (sublane >> (i - low_bits) if i < lane_bit else lane >> (i - lane_bit)) & 1

    held = None
    for level in range(1, total_bits + 1):
        turned = [0] * count
        spread = None
        for at in (held, level):
            if at is None or at >= total_bits:
                continue
            if at < low_bits:
                turned = [turned[t] ^ (t >> at & 1) for t in range(count)]
            else:
                spread = bit(at) if spread is None else spread ^ bit(at)
        for t in range(count):
            if spread is not None:
                tiles[t] = tiles[t] ^ (~(-spread) if turned[t] else -spread)
            elif turned[t]:
                tiles[t] = ~tiles[t]
        held = level
        for j in range(level - 1, -1, -1):
            if j < low_bits:
                for t in range(count):
                    if not t >> j & 1:
                        u = t | 1 << j
                        tiles[t], tiles[u] = (
                            jnp.minimum(tiles[t], tiles[u]),
                            jnp.maximum(tiles[t], tiles[u]),
                        )
                continue
            axis, length, step = (
                (0, SUBLANES, 1 << (j - low_bits))
                if j < lane_bit
                else (1, LANES, 1 << (j - lane_bit))
            )
            low = bit(j) == 0
            for t in range(count):
                other = jnp.where(
                    low, pltpu.roll(tiles[t], length - step, axis), pltpu.roll(tiles[t], step, axis)
                )
                tiles[t] = jnp.where(
                    low, jnp.minimum(tiles[t], other), jnp.maximum(tiles[t], other)
                )
    return tiles


def in_order(tiles, scratch):
    count = len(tiles)
    for t in range(count):
        scratch[pl.ds(t * SUBLANES, SUBLANES), :] = tiles[t]
    whole = jnp.concatenate(
        [scratch[pl.ds(s, count, stride=SUBLANES), :] for s in range(SUBLANES)], axis=0
    )
    return [whole[i * LANES : (i + 1) * LANES].T for i in range(count * SUBLANES // LANES)]


def tiles_for(entries):
    tiles = 16
    while tiles * SUBLANES * LANES < entries:
        tiles *= 2
    return tiles


def cut_windows(group_size, mats, row_count, source_count, window_rows, fused, refs, sent, out):
    keys = refs[0][...]
    small_span = row_count * source_count
    span = mats * small_span if fused else mats
    lane = lax.broadcasted_iota(jnp.int32, (window_rows, LANES), 1)
    place = lax.broadcasted_iota(jnp.int32, (window_rows, LANES), 0) * LANES + lane
    lists = 3 * group_size
    starts = [jnp.sum((keys < k * span).astype(jnp.int32)) for k in range(lists + 1)]
    for k in range(lists):
        length = starts[k + 1] - starts[k]
        front = digits(length + 1, 2)[0]
        for half, (start, size) in enumerate(
            ((starts[k], front), (starts[k] + front, length - front))
        ):
            line, shift = digits(start, LANES)
            turn = digits(LANES - shift, LANES)[1]

            def taken(ref):
                first = ref[pl.ds(line, window_rows), :]
                second = ref[pl.ds(line + 1, window_rows), :]
                return jnp.where(
                    lane < LANES - shift, pltpu.roll(first, turn, 1), pltpu.roll(second, turn, 1)
                )

            if fused:
                large, small = digits(taken(refs[0]), small_span)
            else:
                large, small = taken(refs[0]), taken(refs[1])
            matrix = jnp.where(place < size, digits(large, mats)[1], -1)
            offset, member = k // group_size, k % group_size
            to = member // 2 * 2 + half
            first = ((to * 3 + offset) * 3 * 2 + member % 2) * window_rows
            first += to * (sent.shape[0] // group_size - 18 * window_rows)
            row, source = digits(small, source_count)
            holder, place_there = digits(source, row_count)
            place_there += (holder >> 1) * row_count
            source = place_there + (holder & 1 ^ half) * (source_count // 2)
            for field, value in enumerate((matrix, row, source)):
                sent[pl.ds(first + field * 2 * window_rows, window_rows), :] = value
    rows = 2 * ROWS
    for i in range(sent.shape[0] // rows):
        out[pl.ds(i * rows, rows), :] = sent[pl.ds(i * rows, rows), :].astype(jnp.int16)


def sort_and_cut_kernel(
    sizes, window_rows, live, block_matrix, owner, row, source, out, sent, scratch, ordered
):
    group_size, mats, row_count, source_count = sizes
    blocks = owner.shape[0]
    sublane = lax.broadcasted_iota(jnp.int32, (SUBLANES, LANES), 0)
    tiles = []
    for t in range(scratch.shape[0] // SUBLANES):
        if t * SUBLANES >= blocks:
            tiles.append(jnp.full((SUBLANES, LANES), NONE, jnp.int32))
            continue
        held = pl.ds(t * SUBLANES, SUBLANES)
        matrix = jnp.zeros((SUBLANES, LANES), jnp.int32)
        for s in range(SUBLANES):
            matrix = jnp.where(sublane == s, block_matrix[t * SUBLANES + s], matrix)
        key = (owner[held, :] * mats + matrix) * row_count + row[held, :]
        key = key * source_count + source[held, :]
        tiles.append(jnp.where(sublane + t * SUBLANES < live[0], key, NONE))
    (ordered[...],) = in_order(ascending(tiles), scratch)
    cut_windows(group_size, mats, row_count, source_count, window_rows, True, [ordered], sent, out)


def cut_kernel(sizes, window_rows, *refs):
    group_size, mats, row_count, source_count = sizes
    cut_windows(
        group_size, mats, row_count, source_count, window_rows, False, refs[:2], refs[3], refs[2]
    )


def split_by_owner(sizes, window_rows, live, block_matrix, owner, row, source):
    group_size, mats, row_count, source_count = sizes
    smem, vmem = pl.BlockSpec(memory_space=pltpu.SMEM), pl.BlockSpec(memory_space=pltpu.VMEM)
    message = -(-18 * window_rows // (2 * ROWS)) * 2 * ROWS
    shape = (group_size * message, LANES)
    out = jax.ShapeDtypeStruct(shape, jnp.int16)
    lists = 3 * group_size
    tiles = tiles_for(owner.size)
    if lists * mats * row_count * source_count < NONE and tiles == LANES // SUBLANES:
        return pl.pallas_call(
            functools.partial(sort_and_cut_kernel, sizes, window_rows),
            out_shape=out,
            in_specs=[smem, smem, vmem, vmem, vmem],
            out_specs=vmem,
            scratch_shapes=[pltpu.VMEM(shape, jnp.int32)]
            + [pltpu.VMEM((tiles * SUBLANES, LANES), jnp.int32)] * 2,
        )(live, block_matrix, owner, row, source)
    alive = jnp.arange(owner.shape[0], dtype=jnp.int32)[:, None] < live[0]
    large = jnp.where(alive, owner * mats + block_matrix[:, None], NONE).reshape(-1)
    small = (row * source_count + source).reshape(-1)
    held = [
        jnp.pad(a.reshape(-1, LANES), ((0, 16), (0, 0)), constant_values=NONE)
        for a in lax.sort((large, small), num_keys=1, is_stable=False)
    ]
    return pl.pallas_call(
        functools.partial(cut_kernel, sizes, window_rows),
        out_shape=out,
        in_specs=[vmem, vmem],
        out_specs=vmem,
        scratch_shapes=[pltpu.VMEM(shape, jnp.int32)],
    )(*held)


def plan(bounds, mats, trash, unit_blocks, shape, names_shape):
    def numbers(shape):
        return lax.broadcasted_iota(jnp.int32, shape, 0) * LANES + lax.broadcasted_iota(
            jnp.int32, shape, 1
        )

    block, number = numbers(shape), numbers(names_shape)
    whole_block = ROWS << PLACE_BITS

    def one_matrix(m, carry):
        unit, codes, names = carry
        j = unit * unit_blocks
        for p in range(PHASES):
            start, end = bounds[p * mats + m], bounds[p * mats + m + 1]
            first = digits(start, ROWS)[0]
            count = jnp.where(end > start, digits(end + ROWS - 1, ROWS)[0] - first, 0)
            code = block * whole_block + ((first - j) * whole_block + ROWS)
            code = jnp.where(block == j, code + (start - first * ROWS << EDGE_BITS), code)
            code = jnp.where(block == j + count - 1, code + (end - (first + count) * ROWS), code)
            codes = jnp.where((block >= j) & (block < j + count), code, codes)
            j = j + count
        last = digits(j + unit_blocks - 1, unit_blocks)[0]
        names = jnp.where((number >= unit) & (last > unit), m, names)
        return last, codes, names

    return lax.fori_loop(
        0,
        mats,
        one_matrix,
        (
            0,
            jnp.full(shape, (trash << PLACE_BITS) + ROWS, jnp.int32),
            jnp.zeros(names_shape, jnp.int32),
        ),
    )


def arrived_keys(sizes, member, arrived, message, window_rows):
    group_size, mats, row_count, source_count = sizes
    span = row_count * source_count
    sublane = lax.broadcasted_iota(jnp.int32, (SUBLANES, LANES), 0)
    beside = digits(sublane, window_rows)[0] ^ member
    tiles = []
    for sender in range(group_size):
        taken = arrived[pl.ds(sender * message, message), :].astype(jnp.int32)
        for offset in range(3):
            matrix, row, source = (
                taken[(offset * 3 + field) * SUBLANES : (offset * 3 + field + 1) * SUBLANES]
                for field in range(3)
            )
            key = ((beside * 3 + offset) * mats + matrix) * span + row * source_count + source
            tiles.append(jnp.where(matrix >= 0, key, NONE))
    return tiles


def order_kernel(
    sizes, parts, trash, window_rows, message,
    member, given, bounds, places, rows, codes, names, units, scratch,
):
    group_size, mats, row_count, source_count = sizes
    count = scratch.shape[0] // SUBLANES
    if message:
        tiles = arrived_keys(sizes, member[0], given, message, window_rows)
    else:
        tiles = [
            given[pl.ds(t * SUBLANES, SUBLANES), :] for t in range(given.shape[0] // SUBLANES)
        ]
    for t, tile in enumerate(tiles):
        scratch[pl.ds(t * SUBLANES, SUBLANES), :] = tile
    kept = len(tiles)

    def mark(p, carry):
        below = [jnp.zeros((SUBLANES, LANES), jnp.int32)] * mats
        for t in range(kept):
            tile = scratch[pl.ds(t * SUBLANES, SUBLANES), :]
            for m in range(mats):
                limit = (p * mats + m) * (row_count * source_count)
                below[m] = below[m] + (tile < limit).astype(jnp.int32)
        for m in range(mats):
            bounds[p * mats + m] = jnp.sum(below[m])
        return carry

    lax.fori_loop(0, PHASES, mark, 0)
    every = jnp.zeros((SUBLANES, LANES), jnp.int32)
    for t in range(kept):
        every = every + (scratch[pl.ds(t * SUBLANES, SUBLANES), :] < NONE).astype(jnp.int32)
    bounds[PHASES * mats] = jnp.sum(every)

    tiles = [scratch[pl.ds(t * SUBLANES, SUBLANES), :] for t in range(kept)]
    tiles += [jnp.full((SUBLANES, LANES), NONE, jnp.int32)] * (count - kept)
    strips = in_order(ascending(tiles), scratch)
    kept = places.shape[0] // len(strips)
    for i, strip in enumerate(strips):
        high, source = digits(strip[:kept], source_count)
        held = pl.ds(i, kept, stride=len(strips))
        places[held, :] = source * parts
        rows[held, :] = digits(high, row_count)[1]
    units[0], codes[...], names[...] = plan(
        bounds, mats, trash, UNIT // ROWS, codes.shape, names.shape
    )


def order_pairs(member, given, sizes, parts, most_pairs, window_rows, message):
    mats = sizes[1]
    tiles = tiles_for(sizes[0] * 6 * window_rows * LANES)
    trash = -(-most_pairs // SPAN) * SPAN
    kept = (trash + SPAN) // LANES
    unit_blocks = UNIT // ROWS
    most_units = -(-(-(-most_pairs // ROWS) + 2 * PHASES * mats) // unit_blocks) + mats + 6
    tile = SUBLANES * LANES
    blocks = (-(-most_units * unit_blocks // tile) * SUBLANES, LANES)
    names = (-(-most_units // tile) * SUBLANES, LANES)
    smem, vmem = pl.BlockSpec(memory_space=pltpu.SMEM), pl.BlockSpec(memory_space=pltpu.VMEM)
    shapes = [(PHASES * mats + 1,), (kept, LANES), (kept, LANES), blocks, names, (1,)]
    return pl.pallas_call(
        functools.partial(order_kernel, sizes, parts, trash, window_rows, message),
        out_shape=[jax.ShapeDtypeStruct(shape, jnp.int32) for shape in shapes],
        in_specs=[smem, vmem],
        out_specs=[smem] + [vmem] * 4 + [smem],
        scratch_shapes=[pltpu.VMEM((tiles * SUBLANES, LANES), jnp.int32)],
    )(member, given)


def field_kernel(
    targets, mats,
    bounds, codes, unit_matrix, all_units, rows, places, near, far, table, before, own, after, theirs,
    sources, wide, staged, gather_a, gather_b, gather_c, gather_d, matrices, records, total_ref, places_sem, staged_sems, sems,
):
    coef_width = table.shape[2]
    units = all_units[0]
    mine = (before, own, after)
    parts = gather_a.shape[0] // UNIT
    padded_width = parts * LANES
    unit_blocks = UNIT // ROWS
    entries = sources.shape[0] - ROWS

    length = staged.shape[1]
    half = near.shape[0] // length
    stretches = 2 * half
    slots = staged.shape[0]

    def stage(i):
        return pltpu.make_async_copy(
            (near if i < half else far).at[pl.ds(i % half * length, length), :],
            staged.at[i % slots],
            staged_sems.at[i % slots],
        )

    listing = pltpu.make_async_copy(places, sources, places_sem)
    listing.start()
    for i in range(min(slots, stretches)):
        stage(i).start()

    def fetch(m):
        return pltpu.make_async_copy(
            table.at[m], matrices.at[m, pl.ds(0, coef_width), :], sems.at[m]
        )

    def start_fetch(m, carry):
        matrices[m, pl.ds(coef_width, padded_width - coef_width), :] = jnp.zeros(
            (padded_width - coef_width, coef_width), jnp.bfloat16
        )
        fetch(m).start()
        return carry

    first_used = unit_matrix[0]
    past_used = jnp.where(units > 0, unit_matrix[jnp.maximum(units, 1) - 1] + 1, first_used)
    lax.fori_loop(first_used, past_used, start_fetch, 0)

    for end in (bounds[0], bounds[PHASES * mats]):

        def clear(i, carry):
            place = pl.multiple_of(i * ROWS, ROWS)
            records[pl.ds(place, ROWS), :] = jnp.zeros((ROWS, coef_width), jnp.bfloat16)
            return carry

        span = digits(end, SPAN)[0]
        lax.fori_loop(span * (SPAN // ROWS), (span + 1) * (SPAN // ROWS), clear, 0)

    for i in range(stretches):
        stage(i).wait()

        def widen(j, carry, i=i):
            taken = staged[i % slots, pl.ds(j * WIDEN, WIDEN), :].astype(jnp.float32)
            first = (i * length + j * WIDEN) * parts
            for k in range(parts):
                piece = taken[:, k * LANES : (k + 1) * LANES]
                short = LANES - piece.shape[1]
                if short > 0:
                    piece = jnp.concatenate([piece, jnp.zeros((WIDEN, short), jnp.float32)], axis=1)
                wide[pl.ds(first + k, WIDEN, stride=parts), :] = piece
            return carry

        lax.fori_loop(0, length // WIDEN, widen, 0)
        if i + slots < stretches:
            stage(i + slots).start()

    views = [sources.at[pl.ds(u, entries)] for u in range(ROWS)]
    row_of = lax.broadcasted_iota(jnp.int32, (ROWS, coef_width), 0)

    def gather(unit, into):
        for b in range(unit_blocks):
            start = codes[unit * unit_blocks + b] >> PLACE_BITS
            for u in range(ROWS):
                place = pl.multiple_of(views[u][start], parts)
                into[pl.ds((b * ROWS + u) * parts, parts), :] = wide[pl.ds(place, parts), :]

    def picked(ref):
        return jnp.concatenate(
            [ref[pl.ds(k, UNIT, stride=parts), :].astype(jnp.bfloat16) for k in range(parts)],
            axis=1,
        )

    def work(unit, held, coming):
        lhs = picked(held)
        gather(unit + 2, coming)
        product = jnp.dot(
            lhs, matrices[unit_matrix[unit]], preferred_element_type=jnp.float32
        ).astype(jnp.bfloat16)
        for b in range(unit_blocks):
            code = codes[unit * unit_blocks + b]
            place = pl.multiple_of(code >> PLACE_BITS, ROWS)
            low, high = code >> EDGE_BITS & EDGE, code & EDGE
            made = (row_of >= low) & (row_of < high)
            records[pl.ds(place, ROWS), :] = jnp.where(
                made, product[b * ROWS : (b + 1) * ROWS], records[pl.ds(place, ROWS), :]
            )

    listing.wait()
    gather(0, gather_a)
    gather(1, gather_b)

    def step(i, fetched):
        needed = jnp.maximum(
            jnp.maximum(
                jnp.maximum(unit_matrix[4 * i], unit_matrix[4 * i + 1]),
                jnp.maximum(unit_matrix[4 * i + 2], unit_matrix[4 * i + 3]),
            )
            + 1,
            fetched,
        )

        def await_one(m, carry):
            fetch(m).wait()
            return carry

        lax.fori_loop(fetched, needed, await_one, 0)
        work(4 * i, gather_a, gather_c)
        work(4 * i + 1, gather_b, gather_d)
        work(4 * i + 2, gather_c, gather_a)
        work(4 * i + 3, gather_d, gather_b)
        return needed

    fetched = lax.fori_loop(0, digits(units + 3, 4)[0], step, first_used)

    def await_rest(m, carry):
        fetch(m).wait()
        return carry

    lax.fori_loop(fetched, past_used, await_rest, 0)

    target = lax.broadcasted_iota(jnp.int32, (targets, LANES), 0)
    lane = lax.broadcasted_iota(jnp.int32, (1, LANES), 1)

    for phase in range(PHASES):
        first, end = bounds[phase * mats], bounds[(phase + 1) * mats]

        def add_span(i, carry):
            places = []
            for k in range(SPAN // LANES):
                line = i * (SPAN // LANES) + k
                number = line * LANES + lane
                chosen = jnp.where(
                    (number >= first) & (number < end), rows[pl.ds(line, 1), :], -1
                )
                places.append((target == chosen).astype(jnp.float32).astype(jnp.bfloat16))
            held = records[pl.ds(pl.multiple_of(i * SPAN, SPAN), SPAN), :]
            total_ref[...] += jnp.dot(
                jnp.concatenate(places, axis=1), held, preferred_element_type=jnp.float32
            )
            return carry

        total_ref[...] = jnp.zeros((targets, coef_width), jnp.float32)
        lax.fori_loop(digits(first, SPAN)[0], digits(end + SPAN - 1, SPAN)[0], add_span, 0)
        if phase < len(mine):
            mine[phase][:, pl.ds(0, coef_width)] = total_ref[...]
        else:
            theirs[phase - len(mine), :, pl.ds(0, coef_width)] = total_ref[...].astype(
                jnp.bfloat16
            )
    rest = padded_width - coef_width
    for out in mine:
        out[:, pl.ds(coef_width, rest)] = jnp.zeros((targets, rest), jnp.float32)
    theirs[:, :, pl.ds(coef_width, rest)] = jnp.zeros((len(mine), targets, rest), jnp.bfloat16)


def near_field(targets, bounds, codes, names, units, places, rows, near, far, table):
    mats, coef_width, _ = table.shape
    parts = -(-coef_width // LANES)
    smem, vmem = pl.BlockSpec(memory_space=pltpu.SMEM), pl.BlockSpec(memory_space=pltpu.VMEM)
    shape = (targets, parts * LANES)
    return pl.pallas_call(
        functools.partial(field_kernel, targets, mats),
        out_shape=[jax.ShapeDtypeStruct(shape, jnp.float32)] * 3
        + [jax.ShapeDtypeStruct((3, *shape), jnp.bfloat16)],
        in_specs=[smem] * 4 + [vmem] + [pl.BlockSpec(memory_space=pl.ANY)] * 4,
        out_specs=[vmem] * 4,
        scratch_shapes=[
            pltpu.SMEM((places.size,), jnp.int32),
            pltpu.VMEM((2 * near.shape[0] * parts, LANES), jnp.float32),
            pltpu.VMEM((4, STAGE, coef_width), jnp.bfloat16),
            pltpu.VMEM((UNIT * parts, LANES), jnp.float32),
            pltpu.VMEM((UNIT * parts, LANES), jnp.float32),
            pltpu.VMEM((UNIT * parts, LANES), jnp.float32),
            pltpu.VMEM((UNIT * parts, LANES), jnp.float32),
            pltpu.VMEM((mats, parts * LANES, coef_width), jnp.bfloat16),
            pltpu.VMEM((rows.size, coef_width), jnp.bfloat16),
            pltpu.VMEM((targets, coef_width), jnp.float32),
            pltpu.SemaphoreType.DMA,
            pltpu.SemaphoreType.DMA((4,)),
            pltpu.SemaphoreType.DMA((mats,)),
        ],
        compiler_params=pltpu.CompilerParams(vmem_limit_bytes=VMEM_BYTES),
    )(
        bounds, codes.reshape(-1), names.reshape(-1), units, rows, places.reshape(-1), near, far, table
    )


def on_device(
    coeffs, t_matrix, trans_table, pair_source, pair_owner, pair_row, block_matrix, block_live
):
    row_count, coef_width = coeffs.shape
    half_width = coef_width // 2
    mats = trans_table.shape[0]
    block_count = block_matrix.shape[0]
    pair_count = pair_source.shape[0]
    group_size = lax.axis_size("group")
    source_count = group_size * row_count
    capacity = pair_count // (2 * group_size)
    most_pairs = 3 * group_size * capacity
    window_rows = -(-((capacity + 1) // 2) // LANES)
    parts = -(-coef_width // LANES)

    shape = (block_count, pair_count // block_count)
    fields = split_by_owner(
        (group_size, mats, row_count, source_count),
        window_rows,
        block_live,
        block_matrix,
        pair_owner.reshape(shape),
        pair_row.reshape(shape),
        pair_source.reshape(shape),
    )
    lined, fields = lax.optimization_barrier((coeffs, fields.reshape(group_size, -1, LANES)))
    fields = lax.all_to_all(fields, "group", split_axis=0, concat_axis=0, tiled=True)
    lines = [list(range(parity, group_size, 2)) for parity in range(2)]
    near = lax.all_gather(lined, "group", axis=0, tiled=True, axis_index_groups=lines)
    near, fields = lax.optimization_barrier((near, fields))
    swap = [(g, g ^ 1) for g in range(group_size)]
    far = lax.ppermute(near.reshape(-1, 64, coef_width), "group", swap).reshape(near.shape)

    member = lax.axis_index("group") % 2
    sizes = (group_size, mats, row_count, source_count)
    message = fields.shape[1]
    if 2 * window_rows == SUBLANES:
        given = fields.reshape(-1, LANES)
    else:
        window = window_rows * LANES
        fields = fields[:, : 18 * window_rows].reshape(group_size, 3, 3, 2, window)
        matrix, row, source = (fields[:, :, field].astype(jnp.int32) for field in range(3))
        beside = jnp.arange(2, dtype=jnp.int32)[None, None, :, None] ^ member
        offset = jnp.arange(3, dtype=jnp.int32)[None, :, None, None]
        key = ((3 * beside + offset) * mats + matrix) * row_count + row
        given = jnp.where(matrix >= 0, key * source_count + source, NONE).reshape(-1, LANES)
        message = 0
    bounds, places, rows, codes, names, units = order_pairs(
        jnp.reshape(member, (1,)), given, sizes, parts, most_pairs, window_rows, message
    )
    before, own, after, theirs = near_field(
        row_count, bounds, codes, names, units, places, rows, near, far, trans_table
    )
    shared = lax.ppermute(theirs, "group", swap).astype(jnp.float32)
    from_after = from_behind((before + shared[0]).astype(jnp.bfloat16), "cluster", -1)
    from_before = from_behind((after + shared[2]).astype(jnp.bfloat16), "cluster", 1)
    incoming = own + shared[1] + from_after.astype(jnp.float32) + from_before.astype(jnp.float32)
    incoming = incoming[:, :coef_width]

    real_in, imag_in = incoming[:, :half_width], incoming[:, half_width:]
    real_t, imag_t = t_matrix[:, :half_width], t_matrix[:, half_width:]
    scattered = jnp.concatenate(
        [real_in * real_t - imag_in * imag_t, real_in * imag_t + imag_in * real_t], axis=1
    )
    return coeffs.astype(jnp.float32) - scattered


def solution(mesh):
    owned = P(("cluster", "group"))
    return jax.shard_map(
        on_device,
        mesh=mesh,
        in_specs=(owned, owned, P(), owned, owned, owned, owned, owned),
        out_specs=owned,
        check_vma=False,
    )
```

```python
import functools

import jax
import jax.numpy as jnp
from jax import lax
from jax.experimental import pallas as pl
from jax.experimental.pallas import tpu as pltpu
from jax.sharding import PartitionSpec as P

LANES = 128
SUBLANES = 8
ROWS = 16
UNIT = 256
SPAN = 512
STAGE = 512
WIDEN = 64
PHASES = 6
EDGE_BITS = 5
EDGE = 2**EDGE_BITS - 1
PLACE_BITS = 2 * EDGE_BITS
NONE = 2**31 - 1
VMEM_BYTES = 60 * 2**20


def from_behind(value, axis, steps):
    count = lax.axis_size(axis)
    pairs = [(source, (source + steps) % count) for source in range(count)]
    return lax.ppermute(value, axis, pairs)


def digits(value, span):
    if span & (span - 1) == 0:
        return value >> (span.bit_length() - 1), value & (span - 1)
    return value // span, value % span


def ascending(tiles):
    tiles = list(tiles)
    count = len(tiles)
    low_bits = count.bit_length() - 1
    lane_bit = low_bits + 3
    total_bits = lane_bit + 7
    sublane = lax.broadcasted_iota(jnp.int32, (SUBLANES, LANES), 0)
    lane = lax.broadcasted_iota(jnp.int32, (SUBLANES, LANES), 1)

    def bit(i):
        return (sublane >> (i - low_bits) if i < lane_bit else lane >> (i - lane_bit)) & 1

    held = None
    for level in range(1, total_bits + 1):
        turned = [0] * count
        spread = None
        for at in (held, level):
            if at is None or at >= total_bits:
                continue
            if at < low_bits:
                turned = [turned[t] ^ (t >> at & 1) for t in range(count)]
            else:
                spread = bit(at) if spread is None else spread ^ bit(at)
        for t in range(count):
            if spread is not None:
                tiles[t] = tiles[t] ^ (~(-spread) if turned[t] else -spread)
            elif turned[t]:
                tiles[t] = ~tiles[t]
        held = level
        for j in range(level - 1, -1, -1):
            if j < low_bits:
                for t in range(count):
                    if not t >> j & 1:
                        u = t | 1 << j
                        tiles[t], tiles[u] = (
                            jnp.minimum(tiles[t], tiles[u]),
                            jnp.maximum(tiles[t], tiles[u]),
                        )
                continue
            axis, length, step = (
                (0, SUBLANES, 1 << (j - low_bits))
                if j < lane_bit
                else (1, LANES, 1 << (j - lane_bit))
            )
            low = bit(j) == 0
            for t in range(count):
                other = jnp.where(
                    low, pltpu.roll(tiles[t], length - step, axis), pltpu.roll(tiles[t], step, axis)
                )
                tiles[t] = jnp.where(
                    low, jnp.minimum(tiles[t], other), jnp.maximum(tiles[t], other)
                )
    return tiles


def in_order(tiles, scratch):
    count = len(tiles)
    for t in range(count):
        scratch[pl.ds(t * SUBLANES, SUBLANES), :] = tiles[t]
    whole = jnp.concatenate(
        [scratch[pl.ds(s, count, stride=SUBLANES), :] for s in range(SUBLANES)], axis=0
    )
    return [whole[i * LANES : (i + 1) * LANES].T for i in range(count * SUBLANES // LANES)]


def tiles_for(entries):
    tiles = 16
    while tiles * SUBLANES * LANES < entries:
        tiles *= 2
    return tiles


def cut_windows(group_size, mats, row_count, source_count, window_rows, fused, refs, sent, out):
    keys = refs[0][...]
    small_span = row_count * source_count
    span = mats * small_span if fused else mats
    lane = lax.broadcasted_iota(jnp.int32, (window_rows, LANES), 1)
    place = lax.broadcasted_iota(jnp.int32, (window_rows, LANES), 0) * LANES + lane
    lists = 3 * group_size
    starts = [jnp.sum((keys < k * span).astype(jnp.int32)) for k in range(lists + 1)]
    for k in range(lists):
        length = starts[k + 1] - starts[k]
        front = digits(length + 1, 2)[0]
        for half, (start, size) in enumerate(
            ((starts[k], front), (starts[k] + front, length - front))
        ):
            line, shift = digits(start, LANES)
            turn = digits(LANES - shift, LANES)[1]

            def taken(ref):
                first = ref[pl.ds(line, window_rows), :]
                second = ref[pl.ds(line + 1, window_rows), :]
                return jnp.where(
                    lane < LANES - shift, pltpu.roll(first, turn, 1), pltpu.roll(second, turn, 1)
                )

            if fused:
                large, small = digits(taken(refs[0]), small_span)
            else:
                large, small = taken(refs[0]), taken(refs[1])
            matrix = jnp.where(place < size, digits(large, mats)[1], -1)
            offset, member = k // group_size, k % group_size
            to = member // 2 * 2 + half
            first = ((to * 3 + offset) * 3 * 2 + member % 2) * window_rows
            first += to * (sent.shape[0] // group_size - 18 * window_rows)
            row, source = digits(small, source_count)
            holder, place_there = digits(source, row_count)
            place_there += (holder >> 1) * row_count
            source = place_there + (holder & 1 ^ half) * (source_count // 2)
            for field, value in enumerate((matrix, row, source)):
                sent[pl.ds(first + field * 2 * window_rows, window_rows), :] = value
    rows = 2 * ROWS
    for i in range(sent.shape[0] // rows):
        out[pl.ds(i * rows, rows), :] = sent[pl.ds(i * rows, rows), :].astype(jnp.int16)


def sort_and_cut_kernel(
    sizes, window_rows, live, block_matrix, owner, row, source, out, sent, scratch, ordered
):
    group_size, mats, row_count, source_count = sizes
    blocks = owner.shape[0]
    sublane = lax.broadcasted_iota(jnp.int32, (SUBLANES, LANES), 0)
    tiles = []
    for t in range(scratch.shape[0] // SUBLANES):
        if t * SUBLANES >= blocks:
            tiles.append(jnp.full((SUBLANES, LANES), NONE, jnp.int32))
            continue
        held = pl.ds(t * SUBLANES, SUBLANES)
        matrix = jnp.zeros((SUBLANES, LANES), jnp.int32)
        for s in range(SUBLANES):
            matrix = jnp.where(sublane == s, block_matrix[t * SUBLANES + s], matrix)
        key = (owner[held, :] * mats + matrix) * row_count + row[held, :]
        key = key * source_count + source[held, :]
        tiles.append(jnp.where(sublane + t * SUBLANES < live[0], key, NONE))
    (ordered[...],) = in_order(ascending(tiles), scratch)
    cut_windows(group_size, mats, row_count, source_count, window_rows, True, [ordered], sent, out)


def cut_kernel(sizes, window_rows, *refs):
    group_size, mats, row_count, source_count = sizes
    cut_windows(
        group_size, mats, row_count, source_count, window_rows, False, refs[:2], refs[3], refs[2]
    )


def split_by_owner(sizes, window_rows, live, block_matrix, owner, row, source):
    group_size, mats, row_count, source_count = sizes
    smem, vmem = pl.BlockSpec(memory_space=pltpu.SMEM), pl.BlockSpec(memory_space=pltpu.VMEM)
    message = -(-18 * window_rows // (2 * ROWS)) * 2 * ROWS
    shape = (group_size * message, LANES)
    out = jax.ShapeDtypeStruct(shape, jnp.int16)
    lists = 3 * group_size
    tiles = tiles_for(owner.size)
    if lists * mats * row_count * source_count < NONE and tiles == LANES // SUBLANES:
        return pl.pallas_call(
            functools.partial(sort_and_cut_kernel, sizes, window_rows),
            out_shape=out,
            in_specs=[smem, smem, vmem, vmem, vmem],
            out_specs=vmem,
            scratch_shapes=[pltpu.VMEM(shape, jnp.int32)]
            + [pltpu.VMEM((tiles * SUBLANES, LANES), jnp.int32)] * 2,
        )(live, block_matrix, owner, row, source)
    alive = jnp.arange(owner.shape[0], dtype=jnp.int32)[:, None] < live[0]
    large = jnp.where(alive, owner * mats + block_matrix[:, None], NONE).reshape(-1)
    small = (row * source_count + source).reshape(-1)
    held = [
        jnp.pad(a.reshape(-1, LANES), ((0, 16), (0, 0)), constant_values=NONE)
        for a in lax.sort((large, small), num_keys=1, is_stable=False)
    ]
    return pl.pallas_call(
        functools.partial(cut_kernel, sizes, window_rows),
        out_shape=out,
        in_specs=[vmem, vmem],
        out_specs=vmem,
        scratch_shapes=[pltpu.VMEM(shape, jnp.int32)],
    )(*held)


def plan(bounds, mats, trash, unit_blocks, shape, names_shape):
    def numbers(shape):
        return lax.broadcasted_iota(jnp.int32, shape, 0) * LANES + lax.broadcasted_iota(
            jnp.int32, shape, 1
        )

    block, number = numbers(shape), numbers(names_shape)
    whole_block = ROWS << PLACE_BITS

    def one_matrix(m, carry):
        unit, codes, names = carry
        j = unit * unit_blocks
        for p in range(PHASES):
            start, end = bounds[p * mats + m], bounds[p * mats + m + 1]
            first = digits(start, ROWS)[0]
            count = jnp.where(end > start, digits(end + ROWS - 1, ROWS)[0] - first, 0)
            code = block * whole_block + ((first - j) * whole_block + ROWS)
            code = jnp.where(block == j, code + (start - first * ROWS << EDGE_BITS), code)
            code = jnp.where(block == j + count - 1, code + (end - (first + count) * ROWS), code)
            codes = jnp.where((block >= j) & (block < j + count), code, codes)
            j = j + count
        last = digits(j + unit_blocks - 1, unit_blocks)[0]
        names = jnp.where((number >= unit) & (last > unit), m, names)
        return last, codes, names

    return lax.fori_loop(
        0,
        mats,
        one_matrix,
        (
            0,
            jnp.full(shape, (trash << PLACE_BITS) + ROWS, jnp.int32),
            jnp.zeros(names_shape, jnp.int32),
        ),
    )


def arrived_keys(sizes, member, arrived, message, window_rows):
    group_size, mats, row_count, source_count = sizes
    span = row_count * source_count
    sublane = lax.broadcasted_iota(jnp.int32, (SUBLANES, LANES), 0)
    beside = digits(sublane, window_rows)[0] ^ member
    tiles = []
    for sender in range(group_size):
        taken = arrived[pl.ds(sender * message, message), :].astype(jnp.int32)
        for offset in range(3):
            matrix, row, source = (
                taken[(offset * 3 + field) * SUBLANES : (offset * 3 + field + 1) * SUBLANES]
                for field in range(3)
            )
            key = ((beside * 3 + offset) * mats + matrix) * span + row * source_count + source
            tiles.append(jnp.where(matrix >= 0, key, NONE))
    return tiles


def order_kernel(
    sizes, parts, trash, window_rows, message,
    member, given, bounds, places, rows, codes, names, units, scratch,
):
    group_size, mats, row_count, source_count = sizes
    count = scratch.shape[0] // SUBLANES
    if message:
        tiles = arrived_keys(sizes, member[0], given, message, window_rows)
    else:
        tiles = [
            given[pl.ds(t * SUBLANES, SUBLANES), :] for t in range(given.shape[0] // SUBLANES)
        ]
    for t, tile in enumerate(tiles):
        scratch[pl.ds(t * SUBLANES, SUBLANES), :] = tile
    kept = len(tiles)

    def mark(p, carry):
        below = [jnp.zeros((SUBLANES, LANES), jnp.int32)] * mats
        for t in range(kept):
            tile = scratch[pl.ds(t * SUBLANES, SUBLANES), :]
            for m in range(mats):
                limit = (p * mats + m) * (row_count * source_count)
                below[m] = below[m] + (tile < limit).astype(jnp.int32)
        for m in range(mats):
            bounds[p * mats + m] = jnp.sum(below[m])
        return carry

    lax.fori_loop(0, PHASES, mark, 0)
    every = jnp.zeros((SUBLANES, LANES), jnp.int32)
    for t in range(kept):
        every = every + (scratch[pl.ds(t * SUBLANES, SUBLANES), :] < NONE).astype(jnp.int32)
    bounds[PHASES * mats] = jnp.sum(every)

    tiles = [scratch[pl.ds(t * SUBLANES, SUBLANES), :] for t in range(kept)]
    tiles += [jnp.full((SUBLANES, LANES), NONE, jnp.int32)] * (count - kept)
    strips = in_order(ascending(tiles), scratch)
    kept = places.shape[0] // len(strips)
    for i, strip in enumerate(strips):
        high, source = digits(strip[:kept], source_count)
        held = pl.ds(i, kept, stride=len(strips))
        places[held, :] = source * parts
        rows[held, :] = digits(high, row_count)[1]
    units[0], codes[...], names[...] = plan(
        bounds, mats, trash, UNIT // ROWS, codes.shape, names.shape
    )


def order_pairs(member, given, sizes, parts, most_pairs, window_rows, message):
    mats = sizes[1]
    tiles = tiles_for(sizes[0] * 6 * window_rows * LANES)
    trash = -(-most_pairs // SPAN) * SPAN
    kept = (trash + SPAN) // LANES
    unit_blocks = UNIT // ROWS
    most_units = -(-(-(-most_pairs // ROWS) + 2 * PHASES * mats) // unit_blocks) + mats + 6
    tile = SUBLANES * LANES
    blocks = (-(-most_units * unit_blocks // tile) * SUBLANES, LANES)
    names = (-(-most_units // tile) * SUBLANES, LANES)
    smem, vmem = pl.BlockSpec(memory_space=pltpu.SMEM), pl.BlockSpec(memory_space=pltpu.VMEM)
    shapes = [(PHASES * mats + 1,), (kept, LANES), (kept, LANES), blocks, names, (1,)]
    return pl.pallas_call(
        functools.partial(order_kernel, sizes, parts, trash, window_rows, message),
        out_shape=[jax.ShapeDtypeStruct(shape, jnp.int32) for shape in shapes],
        in_specs=[smem, vmem],
        out_specs=[smem] + [vmem] * 4 + [smem],
        scratch_shapes=[pltpu.VMEM((tiles * SUBLANES, LANES), jnp.int32)],
    )(member, given)


def field_kernel(
    targets, mats,
    bounds, codes, unit_matrix, all_units, rows, places, near, far, table, before, own, after, theirs,
    sources, wide, staged, gather_a, gather_b, gather_c, gather_d, matrices, records, total_ref, places_sem, staged_sems, sems,
):
    coef_width = table.shape[2]
    units = all_units[0]
    mine = (before, own, after)
    parts = gather_a.shape[0] // UNIT
    padded_width = parts * LANES
    unit_blocks = UNIT // ROWS
    entries = sources.shape[0] - ROWS

    length = staged.shape[1]
    half = near.shape[0] // length
    stretches = 2 * half
    slots = staged.shape[0]

    def stage(i):
        return pltpu.make_async_copy(
            (near if i < half else far).at[pl.ds(i % half * length, length), :],
            staged.at[i % slots],
            staged_sems.at[i % slots],
        )

    listing = pltpu.make_async_copy(places, sources, places_sem)
    listing.start()
    for i in range(min(slots, stretches)):
        stage(i).start()

    def fetch(m):
        return pltpu.make_async_copy(
            table.at[m], matrices.at[m, pl.ds(0, coef_width), :], sems.at[m]
        )

    def start_fetch(m, carry):
        matrices[m, pl.ds(coef_width, padded_width - coef_width), :] = jnp.zeros(
            (padded_width - coef_width, coef_width), jnp.bfloat16
        )
        fetch(m).start()
        return carry

    first_used = unit_matrix[0]
    past_used = jnp.where(units > 0, unit_matrix[jnp.maximum(units, 1) - 1] + 1, first_used)
    lax.fori_loop(first_used, past_used, start_fetch, 0)

    for end in (bounds[0], bounds[PHASES * mats]):

        def clear(i, carry):
            place = pl.multiple_of(i * ROWS, ROWS)
            records[pl.ds(place, ROWS), :] = jnp.zeros((ROWS, coef_width), jnp.bfloat16)
            return carry

        span = digits(end, SPAN)[0]
        lax.fori_loop(span * (SPAN // ROWS), (span + 1) * (SPAN // ROWS), clear, 0)

    for i in range(stretches):
        stage(i).wait()

        def widen(j, carry, i=i):
            taken = staged[i % slots, pl.ds(j * WIDEN, WIDEN), :].astype(jnp.float32)
            first = (i * length + j * WIDEN) * parts
            for k in range(parts):
                piece = taken[:, k * LANES : (k + 1) * LANES]
                short = LANES - piece.shape[1]
                if short > 0:
                    piece = jnp.concatenate([piece, jnp.zeros((WIDEN, short), jnp.float32)], axis=1)
                wide[pl.ds(first + k, WIDEN, stride=parts), :] = piece
            return carry

        lax.fori_loop(0, length // WIDEN, widen, 0)
        if i + slots < stretches:
            stage(i + slots).start()

    views = [sources.at[pl.ds(u, entries)] for u in range(ROWS)]
    row_of = lax.broadcasted_iota(jnp.int32, (ROWS, coef_width), 0)

    def gather(unit, into):
        for b in range(unit_blocks):
            start = codes[unit * unit_blocks + b] >> PLACE_BITS
            for u in range(ROWS):
                place = pl.multiple_of(views[u][start], parts)
                into[pl.ds((b * ROWS + u) * parts, parts), :] = wide[pl.ds(place, parts), :]

    def picked(ref):
        return jnp.concatenate(
            [ref[pl.ds(k, UNIT, stride=parts), :].astype(jnp.bfloat16) for k in range(parts)],
            axis=1,
        )

    def work(unit, held, coming):
        lhs = picked(held)
        gather(unit + 2, coming)
        product = jnp.dot(
            lhs, matrices[unit_matrix[unit]], preferred_element_type=jnp.float32
        ).astype(jnp.bfloat16)
        for b in range(unit_blocks):
            code = codes[unit * unit_blocks + b]
            place = pl.multiple_of(code >> PLACE_BITS, ROWS)
            low, high = code >> EDGE_BITS & EDGE, code & EDGE
            made = (row_of >= low) & (row_of < high)
            records[pl.ds(place, ROWS), :] = jnp.where(
                made, product[b * ROWS : (b + 1) * ROWS], records[pl.ds(place, ROWS), :]
            )

    listing.wait()
    gather(0, gather_a)
    gather(1, gather_b)

    def step(i, fetched):
        needed = jnp.maximum(
            jnp.maximum(
                jnp.maximum(unit_matrix[4 * i], unit_matrix[4 * i + 1]),
                jnp.maximum(unit_matrix[4 * i + 2], unit_matrix[4 * i + 3]),
            )
            + 1,
            fetched,
        )

        def await_one(m, carry):
            fetch(m).wait()
            return carry

        lax.fori_loop(fetched, needed, await_one, 0)
        work(4 * i, gather_a, gather_c)
        work(4 * i + 1, gather_b, gather_d)
        work(4 * i + 2, gather_c, gather_a)
        work(4 * i + 3, gather_d, gather_b)
        return needed

    fetched = lax.fori_loop(0, digits(units + 3, 4)[0], step, first_used)

    def await_rest(m, carry):
        fetch(m).wait()
        return carry

    lax.fori_loop(fetched, past_used, await_rest, 0)

    target = lax.broadcasted_iota(jnp.int32, (targets, LANES), 0)
    lane = lax.broadcasted_iota(jnp.int32, (1, LANES), 1)

    for phase in range(PHASES):
        first, end = bounds[phase * mats], bounds[(phase + 1) * mats]

        def add_span(i, carry):
            places = []
            for k in range(SPAN // LANES):
                line = i * (SPAN // LANES) + k
                number = line * LANES + lane
                chosen = jnp.where(
                    (number >= first) & (number < end), rows[pl.ds(line, 1), :], -1
                )
                places.append((target == chosen).astype(jnp.float32).astype(jnp.bfloat16))
            held = records[pl.ds(pl.multiple_of(i * SPAN, SPAN), SPAN), :]
            total_ref[...] += jnp.dot(
                jnp.concatenate(places, axis=1), held, preferred_element_type=jnp.float32
            )
            return carry

        total_ref[...] = jnp.zeros((targets, coef_width), jnp.float32)
        lax.fori_loop(digits(first, SPAN)[0], digits(end + SPAN - 1, SPAN)[0], add_span, 0)
        if phase < len(mine):
            mine[phase][:, pl.ds(0, coef_width)] = total_ref[...]
        else:
            theirs[phase - len(mine), :, pl.ds(0, coef_width)] = total_ref[...].astype(
                jnp.bfloat16
            )
    rest = padded_width - coef_width
    for out in mine:
        out[:, pl.ds(coef_width, rest)] = jnp.zeros((targets, rest), jnp.float32)
    theirs[:, :, pl.ds(coef_width, rest)] = jnp.zeros((len(mine), targets, rest), jnp.bfloat16)


def near_field(targets, bounds, codes, names, units, places, rows, near, far, table):
    mats, coef_width, _ = table.shape
    parts = -(-coef_width // LANES)
    smem, vmem = pl.BlockSpec(memory_space=pltpu.SMEM), pl.BlockSpec(memory_space=pltpu.VMEM)
    shape = (targets, parts * LANES)
    lanes = parts * LANES
    held = 4 * 2 * near.shape[0] * lanes + 2 * lanes * (4 * STAGE + mats * lanes + rows.size)
    held += 4 * lanes * (4 * UNIT + targets)
    sums = 4 * 3 * targets * lanes + 2 * 3 * targets * lanes
    limit = held + sums + 4 * 2**20
    roomy = limit + sums + 2 * far.size < VMEM_BYTES
    if roomy:
        far = pltpu.with_memory_space_constraint(far, pltpu.VMEM)
    sums = pltpu.VMEM if roomy else jax.ShapeDtypeStruct
    return pl.pallas_call(
        functools.partial(field_kernel, targets, mats),
        out_shape=[sums(shape, jnp.float32)] * 3 + [sums((3, *shape), jnp.bfloat16)],
        in_specs=[smem] * 4 + [vmem] + [pl.BlockSpec(memory_space=pl.ANY)] * 4,
        out_specs=[vmem] * 4,
        scratch_shapes=[
            pltpu.SMEM((places.size,), jnp.int32),
            pltpu.VMEM((2 * near.shape[0] * parts, LANES), jnp.float32),
            pltpu.VMEM((4, STAGE, coef_width), jnp.bfloat16),
            pltpu.VMEM((UNIT * parts, LANES), jnp.float32),
            pltpu.VMEM((UNIT * parts, LANES), jnp.float32),
            pltpu.VMEM((UNIT * parts, LANES), jnp.float32),
            pltpu.VMEM((UNIT * parts, LANES), jnp.float32),
            pltpu.VMEM((mats, parts * LANES, coef_width), jnp.bfloat16),
            pltpu.VMEM((rows.size, coef_width), jnp.bfloat16),
            pltpu.VMEM((targets, coef_width), jnp.float32),
            pltpu.SemaphoreType.DMA,
            pltpu.SemaphoreType.DMA((4,)),
            pltpu.SemaphoreType.DMA((mats,)),
        ],
        compiler_params=pltpu.CompilerParams(vmem_limit_bytes=min(limit, VMEM_BYTES)),
    )(
        bounds, codes.reshape(-1), names.reshape(-1), units, rows, places.reshape(-1), near, far, table
    )


def on_device(
    coeffs, t_matrix, trans_table, pair_source, pair_owner, pair_row, block_matrix, block_live
):
    row_count, coef_width = coeffs.shape
    half_width = coef_width // 2
    mats = trans_table.shape[0]
    block_count = block_matrix.shape[0]
    pair_count = pair_source.shape[0]
    group_size = lax.axis_size("group")
    source_count = group_size * row_count
    capacity = pair_count // (2 * group_size)
    most_pairs = 3 * group_size * capacity
    window_rows = -(-((capacity + 1) // 2) // LANES)
    parts = -(-coef_width // LANES)

    shape = (block_count, pair_count // block_count)
    fields = split_by_owner(
        (group_size, mats, row_count, source_count),
        window_rows,
        block_live,
        block_matrix,
        pair_owner.reshape(shape),
        pair_row.reshape(shape),
        pair_source.reshape(shape),
    )
    lined, fields = lax.optimization_barrier((coeffs, fields.reshape(group_size, -1, LANES)))
    fields = lax.all_to_all(fields, "group", split_axis=0, concat_axis=0, tiled=True)
    lines = [list(range(parity, group_size, 2)) for parity in range(2)]
    near = lax.all_gather(lined, "group", axis=0, tiled=True, axis_index_groups=lines)
    near, fields = lax.optimization_barrier((near, fields))
    swap = [(g, g ^ 1) for g in range(group_size)]
    far = lax.ppermute(near.reshape(-1, 64, coef_width), "group", swap).reshape(near.shape)

    member = lax.axis_index("group") % 2
    sizes = (group_size, mats, row_count, source_count)
    message = fields.shape[1]
    if 2 * window_rows == SUBLANES:
        given = pltpu.with_memory_space_constraint(fields.reshape(-1, LANES), pltpu.VMEM)
    else:
        window = window_rows * LANES
        fields = fields[:, : 18 * window_rows].reshape(group_size, 3, 3, 2, window)
        matrix, row, source = (fields[:, :, field].astype(jnp.int32) for field in range(3))
        beside = jnp.arange(2, dtype=jnp.int32)[None, None, :, None] ^ member
        offset = jnp.arange(3, dtype=jnp.int32)[None, :, None, None]
        key = ((3 * beside + offset) * mats + matrix) * row_count + row
        given = jnp.where(matrix >= 0, key * source_count + source, NONE).reshape(-1, LANES)
        message = 0
    bounds, places, rows, codes, names, units = order_pairs(
        jnp.reshape(member, (1,)), given, sizes, parts, most_pairs, window_rows, message
    )
    before, own, after, theirs = near_field(
        row_count, bounds, codes, names, units, places, rows, near, far, trans_table
    )
    shared = lax.ppermute(theirs, "group", swap).astype(jnp.float32)
    from_after = from_behind((before + shared[0]).astype(jnp.bfloat16), "cluster", -1)
    from_before = from_behind((after + shared[2]).astype(jnp.bfloat16), "cluster", 1)
    incoming = own + shared[1] + from_after.astype(jnp.float32) + from_before.astype(jnp.float32)
    incoming = incoming[:, :coef_width]

    real_in, imag_in = incoming[:, :half_width], incoming[:, half_width:]
    real_t, imag_t = t_matrix[:, :half_width], t_matrix[:, half_width:]
    scattered = jnp.concatenate(
        [real_in * real_t - imag_in * imag_t, real_in * imag_t + imag_in * real_t], axis=1
    )
    return coeffs.astype(jnp.float32) - scattered


def solution(mesh):
    owned = P(("cluster", "group"))
    return jax.shard_map(
        on_device,
        mesh=mesh,
        in_specs=(owned, owned, P(), owned, owned, owned, owned, owned),
        out_specs=owned,
        check_vma=False,
    )
```

```python
import functools

import jax
import jax.numpy as jnp
from jax import lax
from jax.experimental import pallas as pl
from jax.experimental.pallas import tpu as pltpu
from jax.sharding import PartitionSpec as P

LANES = 128
SUBLANES = 8
ROWS = 16
UNIT = 256
SPAN = 768
STAGE = 512
WIDEN = 64
PHASES = 6
EDGE_BITS = 5
EDGE = 2**EDGE_BITS - 1
PLACE_BITS = 2 * EDGE_BITS
NONE = 2**31 - 1
VMEM_BYTES = 60 * 2**20


def from_behind(value, axis, steps):
    count = lax.axis_size(axis)
    pairs = [(source, (source + steps) % count) for source in range(count)]
    return lax.ppermute(value, axis, pairs)


def digits(value, span):
    if span & (span - 1) == 0:
        return value >> (span.bit_length() - 1), value & (span - 1)
    return value // span, value % span


def ascending(tiles):
    tiles = list(tiles)
    count = len(tiles)
    low_bits = count.bit_length() - 1
    lane_bit = low_bits + 3
    total_bits = lane_bit + 7
    sublane = lax.broadcasted_iota(jnp.int32, (SUBLANES, LANES), 0)
    lane = lax.broadcasted_iota(jnp.int32, (SUBLANES, LANES), 1)

    def bit(i):
        return (sublane >> (i - low_bits) if i < lane_bit else lane >> (i - lane_bit)) & 1

    held = None
    for level in range(1, total_bits + 1):
        turned = [0] * count
        spread = None
        for at in (held, level):
            if at is None or at >= total_bits:
                continue
            if at < low_bits:
                turned = [turned[t] ^ (t >> at & 1) for t in range(count)]
            else:
                spread = bit(at) if spread is None else spread ^ bit(at)
        for t in range(count):
            if spread is not None:
                tiles[t] = tiles[t] ^ (~(-spread) if turned[t] else -spread)
            elif turned[t]:
                tiles[t] = ~tiles[t]
        held = level
        for j in range(level - 1, -1, -1):
            if j < low_bits:
                for t in range(count):
                    if not t >> j & 1:
                        u = t | 1 << j
                        tiles[t], tiles[u] = (
                            jnp.minimum(tiles[t], tiles[u]),
                            jnp.maximum(tiles[t], tiles[u]),
                        )
                continue
            axis, length, step = (
                (0, SUBLANES, 1 << (j - low_bits))
                if j < lane_bit
                else (1, LANES, 1 << (j - lane_bit))
            )
            low = bit(j) == 0
            for t in range(count):
                other = jnp.where(
                    low, pltpu.roll(tiles[t], length - step, axis), pltpu.roll(tiles[t], step, axis)
                )
                tiles[t] = jnp.where(
                    low, jnp.minimum(tiles[t], other), jnp.maximum(tiles[t], other)
                )
    return tiles


def in_order(tiles, scratch):
    count = len(tiles)
    for t in range(count):
        scratch[pl.ds(t * SUBLANES, SUBLANES), :] = tiles[t]
    whole = jnp.concatenate(
        [scratch[pl.ds(s, count, stride=SUBLANES), :] for s in range(SUBLANES)], axis=0
    )
    return [whole[i * LANES : (i + 1) * LANES].T for i in range(count * SUBLANES // LANES)]


def tiles_for(entries):
    tiles = 16
    while tiles * SUBLANES * LANES < entries:
        tiles *= 2
    return tiles


def cut_windows(group_size, mats, row_count, source_count, window_rows, fused, refs, sent, out):
    keys = refs[0][...]
    small_span = row_count * source_count
    span = mats * small_span if fused else mats
    lane = lax.broadcasted_iota(jnp.int32, (window_rows, LANES), 1)
    place = lax.broadcasted_iota(jnp.int32, (window_rows, LANES), 0) * LANES + lane
    lists = 3 * group_size
    starts = [jnp.sum((keys < k * span).astype(jnp.int32)) for k in range(lists + 1)]
    for k in range(lists):
        length = starts[k + 1] - starts[k]
        front = digits(length + 1, 2)[0]
        for half, (start, size) in enumerate(
            ((starts[k], front), (starts[k] + front, length - front))
        ):
            line, shift = digits(start, LANES)
            turn = digits(LANES - shift, LANES)[1]

            def taken(ref):
                first = ref[pl.ds(line, window_rows), :]
                second = ref[pl.ds(line + 1, window_rows), :]
                return jnp.where(
                    lane < LANES - shift, pltpu.roll(first, turn, 1), pltpu.roll(second, turn, 1)
                )

            if fused:
                large, small = digits(taken(refs[0]), small_span)
            else:
                large, small = taken(refs[0]), taken(refs[1])
            matrix = jnp.where(place < size, digits(large, mats)[1], -1)
            offset, member = k // group_size, k % group_size
            to = member // 2 * 2 + half
            first = ((to * 3 + offset) * 3 * 2 + member % 2) * window_rows
            first += to * (sent.shape[0] // group_size - 18 * window_rows)
            row, source = digits(small, source_count)
            holder, place_there = digits(source, row_count)
            place_there += (holder >> 1) * row_count
            source = place_there + (holder & 1 ^ half) * (source_count // 2)
            for field, value in enumerate((matrix, row, source)):
                sent[pl.ds(first + field * 2 * window_rows, window_rows), :] = value
    rows = 2 * ROWS
    for i in range(sent.shape[0] // rows):
        out[pl.ds(i * rows, rows), :] = sent[pl.ds(i * rows, rows), :].astype(jnp.int16)


def sort_and_cut_kernel(
    sizes, window_rows, live, block_matrix, owner, row, source, out, sent, scratch, ordered
):
    group_size, mats, row_count, source_count = sizes
    blocks = owner.shape[0]
    sublane = lax.broadcasted_iota(jnp.int32, (SUBLANES, LANES), 0)
    tiles = []
    for t in range(scratch.shape[0] // SUBLANES):
        if t * SUBLANES >= blocks:
            tiles.append(jnp.full((SUBLANES, LANES), NONE, jnp.int32))
            continue
        held = pl.ds(t * SUBLANES, SUBLANES)
        matrix = jnp.zeros((SUBLANES, LANES), jnp.int32)
        for s in range(SUBLANES):
            matrix = jnp.where(sublane == s, block_matrix[t * SUBLANES + s], matrix)
        key = (owner[held, :] * mats + matrix) * row_count + row[held, :]
        key = key * source_count + source[held, :]
        tiles.append(jnp.where(sublane + t * SUBLANES < live[0], key, NONE))
    (ordered[...],) = in_order(ascending(tiles), scratch)
    cut_windows(group_size, mats, row_count, source_count, window_rows, True, [ordered], sent, out)


def cut_kernel(sizes, window_rows, *refs):
    group_size, mats, row_count, source_count = sizes
    cut_windows(
        group_size, mats, row_count, source_count, window_rows, False, refs[:2], refs[3], refs[2]
    )


def split_by_owner(sizes, window_rows, live, block_matrix, owner, row, source):
    group_size, mats, row_count, source_count = sizes
    smem, vmem = pl.BlockSpec(memory_space=pltpu.SMEM), pl.BlockSpec(memory_space=pltpu.VMEM)
    message = -(-18 * window_rows // (2 * ROWS)) * 2 * ROWS
    shape = (group_size * message, LANES)
    out = jax.ShapeDtypeStruct(shape, jnp.int16)
    lists = 3 * group_size
    tiles = tiles_for(owner.size)
    if lists * mats * row_count * source_count < NONE and tiles == LANES // SUBLANES:
        return pl.pallas_call(
            functools.partial(sort_and_cut_kernel, sizes, window_rows),
            out_shape=out,
            in_specs=[smem, smem, vmem, vmem, vmem],
            out_specs=vmem,
            scratch_shapes=[pltpu.VMEM(shape, jnp.int32)]
            + [pltpu.VMEM((tiles * SUBLANES, LANES), jnp.int32)] * 2,
        )(live, block_matrix, owner, row, source)
    alive = jnp.arange(owner.shape[0], dtype=jnp.int32)[:, None] < live[0]
    large = jnp.where(alive, owner * mats + block_matrix[:, None], NONE).reshape(-1)
    small = (row * source_count + source).reshape(-1)
    held = [
        jnp.pad(a.reshape(-1, LANES), ((0, 16), (0, 0)), constant_values=NONE)
        for a in lax.sort((large, small), num_keys=1, is_stable=False)
    ]
    return pl.pallas_call(
        functools.partial(cut_kernel, sizes, window_rows),
        out_shape=out,
        in_specs=[vmem, vmem],
        out_specs=vmem,
        scratch_shapes=[pltpu.VMEM(shape, jnp.int32)],
    )(*held)


def plan(bounds, mats, trash, unit_blocks, shape, names_shape):
    def numbers(shape):
        return lax.broadcasted_iota(jnp.int32, shape, 0) * LANES + lax.broadcasted_iota(
            jnp.int32, shape, 1
        )

    block, number = numbers(shape), numbers(names_shape)
    whole_block = ROWS << PLACE_BITS

    def one_matrix(m, carry):
        unit, codes, names = carry
        j = unit * unit_blocks
        for p in range(PHASES):
            start, end = bounds[p * mats + m], bounds[p * mats + m + 1]
            first = digits(start, ROWS)[0]
            count = jnp.where(end > start, digits(end + ROWS - 1, ROWS)[0] - first, 0)
            code = block * whole_block + ((first - j) * whole_block + ROWS)
            code = jnp.where(block == j, code + (start - first * ROWS << EDGE_BITS), code)
            code = jnp.where(block == j + count - 1, code + (end - (first + count) * ROWS), code)
            codes = jnp.where((block >= j) & (block < j + count), code, codes)
            j = j + count
        last = digits(j + unit_blocks - 1, unit_blocks)[0]
        names = jnp.where((number >= unit) & (last > unit), m, names)
        return last, codes, names

    return lax.fori_loop(
        0,
        mats,
        one_matrix,
        (
            0,
            jnp.full(shape, (trash << PLACE_BITS) + ROWS, jnp.int32),
            jnp.zeros(names_shape, jnp.int32),
        ),
    )


def phase_of(offset, beside):
    return 3 * beside + offset


def arrived_keys(sizes, member, arrived, message, window_rows):
    group_size, mats, row_count, source_count = sizes
    span = row_count * source_count
    sublane = lax.broadcasted_iota(jnp.int32, (SUBLANES, LANES), 0)
    beside = digits(sublane, window_rows)[0] ^ member
    tiles = [[], [], []]
    for sender in range(group_size):
        taken = arrived[pl.ds(sender * message, message), :].astype(jnp.int32)
        for offset in range(3):
            matrix, row, source = (
                taken[(offset * 3 + field) * SUBLANES : (offset * 3 + field + 1) * SUBLANES]
                for field in range(3)
            )
            key = (phase_of(offset, beside) * mats + matrix) * span + row * source_count + source
            tiles[offset].append(jnp.where(matrix >= 0, key, NONE))
    return tiles[0] + tiles[1] + tiles[2]


def count_below(scratch, tiles, limits):
    below = [jnp.zeros((SUBLANES, LANES), jnp.int32)] * len(limits)
    for t in tiles:
        tile = scratch[pl.ds(t * SUBLANES, SUBLANES), :]
        for i, limit in enumerate(limits):
            below[i] = below[i] + (tile < limit).astype(jnp.int32)
    return [jnp.sum(each) for each in below]


def order_kernel(
    sizes, parts, trash, window_rows, message,
    member, given, bounds, places, rows, codes, names, units, scratch,
):
    group_size, mats, row_count, source_count = sizes
    count = scratch.shape[0] // SUBLANES
    if message:
        tiles = arrived_keys(sizes, member[0], given, message, window_rows)
    else:
        tiles = [
            given[pl.ds(t * SUBLANES, SUBLANES), :] for t in range(given.shape[0] // SUBLANES)
        ]
    for t, tile in enumerate(tiles):
        scratch[pl.ds(t * SUBLANES, SUBLANES), :] = tile
    kept = len(tiles)

    span = row_count * source_count
    if message:
        sizes_of, within = [0] * PHASES, [None] * PHASES
        for offset in range(3):
            held = range(offset * group_size, (offset + 1) * group_size)
            low, high = sorted((phase_of(offset, 0), phase_of(offset, 1)))
            ends = count_below(scratch, held, [(low + 1) * mats * span, NONE])
            sizes_of[low], sizes_of[high] = ends[0], ends[1] - ends[0]
            for p, less in ((low, 0), (high, ends[0])):
                marks = [(p * mats + m) * span for m in range(mats)]
                within[p] = [n - less for n in count_below(scratch, held, marks)]
        first = 0
        for p in range(PHASES):
            for m in range(mats):
                bounds[p * mats + m] = first + within[p][m]
            first = first + sizes_of[p]
        bounds[PHASES * mats] = first
    else:

        def mark(p, carry):
            marks = [(p * mats + m) * span for m in range(mats)]
            for m, n in enumerate(count_below(scratch, range(kept), marks)):
                bounds[p * mats + m] = n
            return carry

        lax.fori_loop(0, PHASES, mark, 0)
        (bounds[PHASES * mats],) = count_below(scratch, range(kept), [NONE])

    tiles = [scratch[pl.ds(t * SUBLANES, SUBLANES), :] for t in range(kept)]
    tiles += [jnp.full((SUBLANES, LANES), NONE, jnp.int32)] * (count - kept)
    strips = in_order(ascending(tiles), scratch)
    kept = places.shape[0] // len(strips)
    for i, strip in enumerate(strips):
        high, source = digits(strip[:kept], source_count)
        held = pl.ds(i, kept, stride=len(strips))
        places[held, :] = source * parts
        rows[held, :] = digits(high, row_count)[1]
    units[0], codes[...], names[...] = plan(
        bounds, mats, trash, UNIT // ROWS, codes.shape, names.shape
    )


def order_pairs(member, given, sizes, parts, most_pairs, window_rows, message):
    mats = sizes[1]
    tiles = tiles_for(sizes[0] * 6 * window_rows * LANES)
    trash = -(-most_pairs // SPAN) * SPAN
    kept = (trash + SPAN) // LANES
    unit_blocks = UNIT // ROWS
    most_units = -(-(-(-most_pairs // ROWS) + 2 * PHASES * mats) // unit_blocks) + mats + 6
    tile = SUBLANES * LANES
    blocks = (-(-most_units * unit_blocks // tile) * SUBLANES, LANES)
    names = (-(-most_units // tile) * SUBLANES, LANES)
    smem, vmem = pl.BlockSpec(memory_space=pltpu.SMEM), pl.BlockSpec(memory_space=pltpu.VMEM)
    shapes = [(PHASES * mats + 1,), (kept, LANES), (kept, LANES), blocks, names, (1,)]
    return pl.pallas_call(
        functools.partial(order_kernel, sizes, parts, trash, window_rows, message),
        out_shape=[jax.ShapeDtypeStruct(shape, jnp.int32) for shape in shapes],
        in_specs=[smem, vmem],
        out_specs=[smem] + [vmem] * 4 + [smem],
        scratch_shapes=[pltpu.VMEM((tiles * SUBLANES, LANES), jnp.int32)],
    )(member, given)


def field_kernel(
    targets, mats,
    bounds, codes, unit_matrix, all_units, rows, places, near, far, table, before, own, after, theirs,
    sources, wide, staged, gather_a, gather_b, gather_c, gather_d, matrices, records, total_ref, places_sem, staged_sems, sems,
):
    coef_width = table.shape[2]
    units = all_units[0]
    mine = (before, own, after)
    parts = gather_a.shape[0] // UNIT
    padded_width = parts * LANES
    unit_blocks = UNIT // ROWS
    entries = sources.shape[0] - ROWS

    length = staged.shape[1]
    half = near.shape[0] // length
    stretches = 2 * half
    slots = staged.shape[0]

    def stage(i):
        return pltpu.make_async_copy(
            (near if i < half else far).at[pl.ds(i % half * length, length), :],
            staged.at[i % slots],
            staged_sems.at[i % slots],
        )

    listing = pltpu.make_async_copy(places, sources, places_sem)
    listing.start()
    for i in range(min(slots, stretches)):
        stage(i).start()

    def fetch(m):
        return pltpu.make_async_copy(
            table.at[m], matrices.at[m, pl.ds(0, coef_width), :], sems.at[m]
        )

    def start_fetch(m, carry):
        matrices[m, pl.ds(coef_width, padded_width - coef_width), :] = jnp.zeros(
            (padded_width - coef_width, coef_width), jnp.bfloat16
        )
        fetch(m).start()
        return carry

    first_used = unit_matrix[0]
    past_used = jnp.where(units > 0, unit_matrix[jnp.maximum(units, 1) - 1] + 1, first_used)
    lax.fori_loop(first_used, past_used, start_fetch, 0)

    for end in (bounds[0], bounds[PHASES * mats]):

        def clear(i, carry):
            place = pl.multiple_of(i * ROWS, ROWS)
            records[pl.ds(place, ROWS), :] = jnp.zeros((ROWS, coef_width), jnp.bfloat16)
            return carry

        span = digits(end, SPAN)[0]
        lax.fori_loop(span * (SPAN // ROWS), (span + 1) * (SPAN // ROWS), clear, 0)

    for i in range(stretches):
        stage(i).wait()

        def widen(j, carry, i=i):
            taken = staged[i % slots, pl.ds(j * WIDEN, WIDEN), :].astype(jnp.float32)
            first = (i * length + j * WIDEN) * parts
            for k in range(parts):
                piece = taken[:, k * LANES : (k + 1) * LANES]
                short = LANES - piece.shape[1]
                if short > 0:
                    piece = jnp.concatenate([piece, jnp.zeros((WIDEN, short), jnp.float32)], axis=1)
                wide[pl.ds(first + k, WIDEN, stride=parts), :] = piece
            return carry

        lax.fori_loop(0, length // WIDEN, widen, 0)
        if i + slots < stretches:
            stage(i + slots).start()

    views = [sources.at[pl.ds(u, entries)] for u in range(ROWS)]
    row_of = lax.broadcasted_iota(jnp.int32, (ROWS, coef_width), 0)

    def gather(unit, into):
        for b in range(unit_blocks):
            start = codes[unit * unit_blocks + b] >> PLACE_BITS
            for u in range(ROWS):
                place = pl.multiple_of(views[u][start], parts)
                into[pl.ds((b * ROWS + u) * parts, parts), :] = wide[pl.ds(place, parts), :]

    def picked(ref):
        return jnp.concatenate(
            [ref[pl.ds(k, UNIT, stride=parts), :].astype(jnp.bfloat16) for k in range(parts)],
            axis=1,
        )

    def work(unit, held, coming):
        lhs = picked(held)
        gather(unit + 2, coming)
        product = jnp.dot(
            lhs, matrices[unit_matrix[unit]], preferred_element_type=jnp.float32
        ).astype(jnp.bfloat16)
        for b in range(unit_blocks):
            code = codes[unit * unit_blocks + b]
            place = pl.multiple_of(code >> PLACE_BITS, ROWS)
            low, high = code >> EDGE_BITS & EDGE, code & EDGE
            made = (row_of >= low) & (row_of < high)
            records[pl.ds(place, ROWS), :] = jnp.where(
                made, product[b * ROWS : (b + 1) * ROWS], records[pl.ds(place, ROWS), :]
            )

    listing.wait()
    gather(0, gather_a)
    gather(1, gather_b)

    def step(i, fetched):
        needed = jnp.maximum(
            jnp.maximum(
                jnp.maximum(unit_matrix[4 * i], unit_matrix[4 * i + 1]),
                jnp.maximum(unit_matrix[4 * i + 2], unit_matrix[4 * i + 3]),
            )
            + 1,
            fetched,
        )

        def await_one(m, carry):
            fetch(m).wait()
            return carry

        lax.fori_loop(fetched, needed, await_one, 0)
        work(4 * i, gather_a, gather_c)
        work(4 * i + 1, gather_b, gather_d)
        work(4 * i + 2, gather_c, gather_a)
        work(4 * i + 3, gather_d, gather_b)
        return needed

    fetched = lax.fori_loop(0, digits(units + 3, 4)[0], step, first_used)

    def await_rest(m, carry):
        fetch(m).wait()
        return carry

    lax.fori_loop(fetched, past_used, await_rest, 0)

    target = lax.broadcasted_iota(jnp.int32, (targets, LANES), 0)
    lane = lax.broadcasted_iota(jnp.int32, (1, LANES), 1)

    for phase in range(PHASES):
        first, end = bounds[phase * mats], bounds[(phase + 1) * mats]

        def add_span(i, carry):
            places = []
            for k in range(SPAN // LANES):
                line = i * (SPAN // LANES) + k
                number = line * LANES + lane
                chosen = jnp.where(
                    (number >= first) & (number < end), rows[pl.ds(line, 1), :], -1
                )
                places.append((target == chosen).astype(jnp.float32).astype(jnp.bfloat16))
            held = records[pl.ds(pl.multiple_of(i * SPAN, SPAN), SPAN), :]
            total_ref[...] += jnp.dot(
                jnp.concatenate(places, axis=1), held, preferred_element_type=jnp.float32
            )
            return carry

        total_ref[...] = jnp.zeros((targets, coef_width), jnp.float32)
        lax.fori_loop(digits(first, SPAN)[0], digits(end + SPAN - 1, SPAN)[0], add_span, 0)
        if phase < len(mine):
            mine[phase][:, pl.ds(0, coef_width)] = total_ref[...]
        else:
            theirs[phase - len(mine), :, pl.ds(0, coef_width)] = total_ref[...].astype(
                jnp.bfloat16
            )
    rest = padded_width - coef_width
    for out in mine:
        out[:, pl.ds(coef_width, rest)] = jnp.zeros((targets, rest), jnp.float32)
    theirs[:, :, pl.ds(coef_width, rest)] = jnp.zeros((len(mine), targets, rest), jnp.bfloat16)


def near_field(targets, bounds, codes, names, units, places, rows, near, far, table):
    mats, coef_width, _ = table.shape
    parts = -(-coef_width // LANES)
    smem, vmem = pl.BlockSpec(memory_space=pltpu.SMEM), pl.BlockSpec(memory_space=pltpu.VMEM)
    shape = (targets, parts * LANES)
    lanes = parts * LANES
    held = 4 * 2 * near.shape[0] * lanes + 2 * lanes * (4 * STAGE + mats * lanes + rows.size)
    held += 4 * lanes * (4 * UNIT + targets)
    sums = 4 * 3 * targets * lanes + 2 * 3 * targets * lanes
    limit = held + sums + 4 * 2**20
    roomy = limit + sums + 2 * far.size < VMEM_BYTES
    if roomy:
        far = pltpu.with_memory_space_constraint(far, pltpu.VMEM)
    sums = pltpu.VMEM if roomy else jax.ShapeDtypeStruct
    return pl.pallas_call(
        functools.partial(field_kernel, targets, mats),
        out_shape=[sums(shape, jnp.float32)] * 3 + [sums((3, *shape), jnp.bfloat16)],
        in_specs=[smem] * 4 + [vmem] + [pl.BlockSpec(memory_space=pl.ANY)] * 4,
        out_specs=[vmem] * 4,
        scratch_shapes=[
            pltpu.SMEM((places.size,), jnp.int32),
            pltpu.VMEM((2 * near.shape[0] * parts, LANES), jnp.float32),
            pltpu.VMEM((4, STAGE, coef_width), jnp.bfloat16),
            pltpu.VMEM((UNIT * parts, LANES), jnp.float32),
            pltpu.VMEM((UNIT * parts, LANES), jnp.float32),
            pltpu.VMEM((UNIT * parts, LANES), jnp.float32),
            pltpu.VMEM((UNIT * parts, LANES), jnp.float32),
            pltpu.VMEM((mats, parts * LANES, coef_width), jnp.bfloat16),
            pltpu.VMEM((rows.size, coef_width), jnp.bfloat16),
            pltpu.VMEM((targets, coef_width), jnp.float32),
            pltpu.SemaphoreType.DMA,
            pltpu.SemaphoreType.DMA((4,)),
            pltpu.SemaphoreType.DMA((mats,)),
        ],
        compiler_params=pltpu.CompilerParams(vmem_limit_bytes=min(limit, VMEM_BYTES)),
    )(
        bounds, codes.reshape(-1), names.reshape(-1), units, rows, places.reshape(-1), near, far, table
    )


def on_device(
    coeffs, t_matrix, trans_table, pair_source, pair_owner, pair_row, block_matrix, block_live
):
    row_count, coef_width = coeffs.shape
    half_width = coef_width // 2
    mats = trans_table.shape[0]
    block_count = block_matrix.shape[0]
    pair_count = pair_source.shape[0]
    group_size = lax.axis_size("group")
    source_count = group_size * row_count
    capacity = pair_count // (2 * group_size)
    most_pairs = 3 * group_size * capacity
    window_rows = -(-((capacity + 1) // 2) // LANES)
    parts = -(-coef_width // LANES)

    shape = (block_count, pair_count // block_count)
    fields = split_by_owner(
        (group_size, mats, row_count, source_count),
        window_rows,
        block_live,
        block_matrix,
        pair_owner.reshape(shape),
        pair_row.reshape(shape),
        pair_source.reshape(shape),
    )
    lined, fields = lax.optimization_barrier((coeffs, fields.reshape(group_size, -1, LANES)))
    fields = lax.all_to_all(fields, "group", split_axis=0, concat_axis=0, tiled=True)
    lines = [list(range(parity, group_size, 2)) for parity in range(2)]
    near = lax.all_gather(lined, "group", axis=0, tiled=True, axis_index_groups=lines)
    near, fields = lax.optimization_barrier((near, fields))
    swap = [(g, g ^ 1) for g in range(group_size)]
    far = lax.ppermute(near.reshape(-1, 64, coef_width), "group", swap).reshape(near.shape)

    member = lax.axis_index("group") % 2
    sizes = (group_size, mats, row_count, source_count)
    message = fields.shape[1]
    if 2 * window_rows == SUBLANES:
        given = pltpu.with_memory_space_constraint(fields.reshape(-1, LANES), pltpu.VMEM)
    else:
        window = window_rows * LANES
        fields = fields[:, : 18 * window_rows].reshape(group_size, 3, 3, 2, window)
        matrix, row, source = (fields[:, :, field].astype(jnp.int32) for field in range(3))
        beside = jnp.arange(2, dtype=jnp.int32)[None, None, :, None] ^ member
        offset = jnp.arange(3, dtype=jnp.int32)[None, :, None, None]
        key = (phase_of(offset, beside) * mats + matrix) * row_count + row
        given = jnp.where(matrix >= 0, key * source_count + source, NONE).reshape(-1, LANES)
        message = 0
    bounds, places, rows, codes, names, units = order_pairs(
        jnp.reshape(member, (1,)), given, sizes, parts, most_pairs, window_rows, message
    )
    before, own, after, theirs = near_field(
        row_count, bounds, codes, names, units, places, rows, near, far, trans_table
    )
    shared = lax.ppermute(theirs, "group", swap).astype(jnp.float32)
    from_after = from_behind((before + shared[0]).astype(jnp.bfloat16), "cluster", -1)
    from_before = from_behind((after + shared[2]).astype(jnp.bfloat16), "cluster", 1)
    incoming = own + shared[1] + from_after.astype(jnp.float32) + from_before.astype(jnp.float32)
    incoming = incoming[:, :coef_width]

    real_in, imag_in = incoming[:, :half_width], incoming[:, half_width:]
    real_t, imag_t = t_matrix[:, :half_width], t_matrix[:, half_width:]
    scattered = jnp.concatenate(
        [real_in * real_t - imag_in * imag_t, real_in * imag_t + imag_in * real_t], axis=1
    )
    return coeffs.astype(jnp.float32) - scattered


def solution(mesh):
    owned = P(("cluster", "group"))
    return jax.shard_map(
        on_device,
        mesh=mesh,
        in_specs=(owned, owned, P(), owned, owned, owned, owned, owned),
        out_specs=owned,
        check_vma=False,
    )
```
